768 devices in a mesh: pb: 12 (over z), pool: 64 (over y, x, core).
Axes of the slice: x: 4, y: 8, z: 12, core: 2. Of those that a mesh axis runs over, the one named last changes fastest.
Arguments:
- queries: bfloat16 [98304, 4096], P(('pb', 'pool')), may hold values from -1 to 1
- passages: bfloat16 [98304, 4096], P(('pb', 'pool')), may hold values from -1 to 1
- pool_passages: bfloat16 [1536, 4096], P(('pb', 'pool')), may hold values from -0.09375 to 0.09375
- positives: int32 [98304], P(('pb', 'pool')), may hold values from 0 to 127
- tile_ids: int32 [12, 64, 12, 2], P('pb', 'pool'), may hold values from 0 to 15
- tile_count: int32 [12, 64, 12], P('pb', 'pool'), may hold values from 1 to 2, as said below
Outputs:
- grad_queries: bfloat16 [98304, 4096], P(('pb', 'pool'))
- grad_passages: bfloat16 [98304, 4096], P(('pb', 'pool'))
- grad_pool: bfloat16 [1536, 4096], P(('pb', 'pool'))
The draws below stay inside these ranges and needn't reach their ends.
Inputs may be any that keep to these rules, and one draw needn't show every extreme that they name: `tile_count`: every entry is at most 2; at some index of pool, one destination receives 2 slots from every source.
All inputs are finite; a program needn't handle non-finite values.
Results may differ from the reference program's by a relative error of at most 0.0041.
Values may be sent and summed in bfloat16 or wider, within the bound.
No kernel may reach another device: no remote copies, remote signals or barrier semaphores. Data moves between devices by JAX's collectives and lax.ppermute only.
A program may use at most 32 MiB of HBM per device.

```python
import math
import jax
import jax.numpy as jnp
from jax import lax

D = 4096
ROWS_DEV = 128
TILE = 8
CAP = 2
POOL_DEV = 2
PTILES = 16
NQ = 98304
POOL_ALL = 1536
N_PB = 12
N_POOL = 64


def embed_pair(key):
    first, second = jax.random.split(key, 2)
    unit = 1.0 / math.sqrt(D)
    passage = jax.random.truncated_normal(first, -6.0, 6.0, (NQ, D), jnp.float32) * unit
    query = jax.random.truncated_normal(second, -6.0, 6.0, (NQ, D), jnp.float32) * unit
    return (jnp.clip(query, -1.0, 1.0), jnp.clip(passage, -1.0, 1.0))


def draw_queries(key, part):
    query, passage = embed_pair(key)
    return query.astype(jnp.bfloat16)


def draw_passages(key, part):
    query, passage = embed_pair(key)
    return passage.astype(jnp.bfloat16)


def draw_tile_count(key, part):
    key = jax.random.fold_in(key, 7)
    first, second, third = jax.random.split(key, 3)
    counts = jax.random.randint(first, (N_PB, N_POOL, N_PB), 1, CAP + 1)
    target = jax.random.randint(second, (), 0, N_PB)
    column = jax.random.randint(third, (), 0, N_POOL)
    full = (jnp.arange(N_PB)[:, None, None] == target) & (jnp.arange(N_POOL)[None, :, None] == column)
    return jnp.where(full, CAP, counts).astype(jnp.int32)


def plant(drawn, stream_key, low, high):
    longest = drawn.shape.index(max(drawn.shape))
    spots = []
    for shift in (0, 1):
        where = [jax.random.randint(jax.random.fold_in(stream_key, axis), (), 0, length) for axis, length in enumerate(drawn.shape)]
        where[longest] = (where[longest] + shift) % drawn.shape[longest]
        spots.append(tuple(where))
    return drawn.at[spots[0]].set(low).at[spots[1]].set(high)


def level_of(own_key, shape, cuts, smallest, high):
    loudness, own = 1.0, jax.random.fold_in(own_key, 6)
    for axis_at, shards_of in cuts:
        draws = jnp.exp(jax.random.uniform(jax.random.fold_in(own, axis_at), (shards_of,), jnp.float32, smallest / len(cuts), high / len(cuts)))
        loudness = loudness * jnp.repeat(draws, shape[axis_at] // shards_of).reshape([-1 if axis == axis_at else 1 for axis in range(len(shape))])
    return loudness


def bell_draw(own_key, extent, scale, reach, cuts=(), held_as=jnp.bfloat16):
    array = jax.random.normal(own_key, extent, jnp.float32) * scale
    if len(cuts) > 0:
        array = level_of(own_key, extent, cuts, -0.22, 0.18) * array
    return jnp.clip(array, min=-reach, max=reach).astype(held_as)


def setup_inputs(seed: int = 0) -> dict:
    key_list = jax.random.split(jax.random.key(seed), 7)
    return {
        "queries": draw_queries(jax.random.fold_in(key_list[6], 71), 0),
        "passages": draw_passages(jax.random.fold_in(key_list[6], 71), 0),
        "pool_passages": bell_draw(key_list[2], (POOL_ALL, D), D ** -0.5, 0.09375, ((0, 768),)),
        "positives": plant(jax.random.randint(key_list[3], (NQ,), 0, ROWS_DEV), jax.random.fold_in(key_list[3], 1), 0, ROWS_DEV - 1).astype(jnp.int32),
        "tile_ids": plant(jax.random.randint(key_list[4], (N_PB, N_POOL, N_PB, CAP), 0, PTILES), jax.random.fold_in(key_list[4], 1), 0, PTILES - 1).astype(jnp.int32),
        "tile_count": draw_tile_count(jax.random.fold_in(key_list[6], 71), 0),
    }


SHARPNESS = 50.0


def contract(left, right):
    return lax.dot_general(left, right, (((1,), (1,)), ((), ())), preferred_element_type=jnp.float32)


def transposed(left, right):
    return lax.dot_general(left, right, (((0,), (0,)), ((), ())), preferred_element_type=jnp.float32)


def device_pass(query_rows, local_rows, positive, pooled, hard_rows, hard_mask):
    local_logit = SHARPNESS * contract(query_rows, local_rows)
    pool_logit = SHARPNESS * contract(query_rows, pooled)
    hard_logit = jnp.where(hard_mask[None, :], SHARPNESS * contract(query_rows, hard_rows), -jnp.inf)
    highest = jnp.maximum(jnp.max(local_logit, axis=1, keepdims=True), jnp.max(pool_logit, axis=1, keepdims=True))
    highest = jnp.maximum(highest, jnp.max(hard_logit, axis=1, keepdims=True))
    local_exp = jnp.exp(local_logit - highest)
    pool_exp = jnp.exp(pool_logit - highest)
    hard_exp = jnp.exp(hard_logit - highest)
    total = jnp.sum(local_exp, axis=1, keepdims=True) + jnp.sum(pool_exp, axis=1, keepdims=True) + jnp.sum(hard_exp, axis=1, keepdims=True)
    target = (positive[:, None] == jnp.arange(local_rows.shape[0], dtype=jnp.int32)[None, :]).astype(jnp.float32)
    local_weight = (local_exp / total - target).astype(jnp.bfloat16)
    pool_weight = (pool_exp / total).astype(jnp.bfloat16)
    hard_weight = (hard_exp / total).astype(jnp.bfloat16)
    grad_query = jnp.dot(local_weight, local_rows, preferred_element_type=jnp.float32)
    grad_query = grad_query + jnp.dot(pool_weight, pooled, preferred_element_type=jnp.float32)
    grad_query = grad_query + jnp.dot(hard_weight, hard_rows, preferred_element_type=jnp.float32)
    grad_query = (SHARPNESS * grad_query).astype(jnp.bfloat16)
    grad_local = SHARPNESS * transposed(local_weight, query_rows)
    grad_pooled = SHARPNESS * transposed(pool_weight, query_rows)
    grad_hard = (SHARPNESS * transposed(hard_weight, query_rows)).astype(jnp.bfloat16)
    return grad_query, grad_local, grad_pooled, grad_hard


def reference(queries, passages, pool_passages, positives, tile_ids, tile_count):
    query_all = queries.reshape(N_PB, N_POOL, ROWS_DEV, D)
    passage_all = passages.reshape(N_PB, N_POOL, ROWS_DEV, D)
    positive_all = positives.reshape(N_PB, N_POOL, ROWS_DEV)
    pool_all = pool_passages.reshape(N_PB, N_POOL * POOL_DEV, D)
    slot_index = jnp.arange(CAP, dtype=jnp.int32)

    def column_step(carry, column):
        query_rows = query_all[:, column]
        local_rows = passage_all[:, column]
        positive = positive_all[:, column]
        picks = tile_ids[:, column]
        counts = tile_count[:, column]
        own_tiles = local_rows.reshape(N_PB, PTILES, TILE, D)
        sent = jax.vmap(lambda owned, chosen: owned[chosen])(own_tiles, picks)
        received = jnp.swapaxes(sent, 0, 1).reshape(N_PB, N_PB * CAP * TILE, D)
        live = slot_index[None, None, :] < counts[:, :, None]
        hard_mask = jnp.broadcast_to(live[:, :, :, None], (N_PB, N_PB, CAP, TILE)).reshape(N_PB, N_PB * CAP * TILE)
        grad_query, grad_local, grad_pooled, grad_hard = jax.vmap(device_pass)(query_rows, local_rows, positive, pool_all, received, hard_mask)
        returned = jnp.swapaxes(grad_hard.reshape(N_PB, N_PB, CAP, TILE, D), 0, 1).reshape(N_PB, N_PB * CAP, TILE, D)
        flat_picks = picks.reshape(N_PB, N_PB * CAP)
        summed = jax.vmap(lambda owned, chosen, grads: owned.at[chosen].add(grads.astype(jnp.float32)))(grad_local.reshape(N_PB, PTILES, TILE, D), flat_picks, returned)
        return carry + grad_pooled, (grad_query, summed.reshape(N_PB, ROWS_DEV, D).astype(jnp.bfloat16))

    start = jnp.zeros((N_PB, N_POOL * POOL_DEV, D), jnp.float32)
    pool_sum, (query_grads, passage_grads) = lax.scan(column_step, start, jnp.arange(N_POOL, dtype=jnp.int32))
    grad_queries = jnp.swapaxes(query_grads, 0, 1).reshape(NQ, D)
    grad_passages = jnp.swapaxes(passage_grads, 0, 1).reshape(NQ, D)
    grad_pool = pool_sum.reshape(POOL_ALL, D).astype(jnp.bfloat16)
    return grad_queries, grad_passages, grad_pool
```

```python
import jax
import jax.numpy as jnp
from jax import lax
from jax.sharding import PartitionSpec as P

TILE = 8


SHARPNESS = 50.0


def contract(left, right):
    return lax.dot_general(
        left, right, (((1,), (1,)), ((), ())), preferred_element_type=jnp.float32
    )


def transposed(left, right):
    return lax.dot_general(
        left, right, (((0,), (0,)), ((), ())), preferred_element_type=jnp.float32
    )


def exchange(block, bit, size):
    return lax.ppermute(block, "pool", [(j, j ^ bit) for j in range(size)])


def body(bits, wide, queries, passages, pool_passages, positives, tile_ids, tile_count):
    rows, width = queries.shape
    picks = tile_ids[0, 0]
    peers, slots = picks.shape
    hard = peers * slots * TILE
    size = 1 << len(bits)
    wanted = (
        picks.reshape(-1)[:, None] * TILE + jnp.arange(TILE, dtype=jnp.int32)[None, :]
    ).reshape(hard)
    chosen = (wanted[:, None] == jnp.arange(rows, dtype=jnp.int32)[None, :]).astype(jnp.bfloat16)
    outgoing = jnp.dot(chosen, passages, preferred_element_type=jnp.float32).astype(jnp.bfloat16)
    hard_rows = lax.all_to_all(
        outgoing.reshape(peers, slots * TILE, width), "pb", split_axis=0, concat_axis=0, tiled=True
    ).reshape(hard, width)
    live = jnp.arange(slots, dtype=jnp.int32)[None, :] < tile_count[0, 0][:, None]
    hard_mask = jnp.broadcast_to(live[:, :, None], (peers, slots, TILE)).reshape(hard)
    pooled = pool_passages
    for bit in bits:
        pooled = jnp.concatenate([pooled, exchange(pooled, bit, size)], axis=0)
    local_logit = SHARPNESS * contract(queries, passages)
    pool_logit = SHARPNESS * contract(queries, pooled)
    hard_logit = jnp.where(hard_mask[None, :], SHARPNESS * contract(queries, hard_rows), -jnp.inf)
    highest = jnp.maximum(
        jnp.max(local_logit, axis=1, keepdims=True), jnp.max(pool_logit, axis=1, keepdims=True)
    )
    highest = jnp.maximum(highest, jnp.max(hard_logit, axis=1, keepdims=True))
    local_exp = jnp.exp(local_logit - highest)
    pool_exp = jnp.exp(pool_logit - highest)
    hard_exp = jnp.exp(hard_logit - highest)
    total = (
        jnp.sum(local_exp, axis=1, keepdims=True)
        + jnp.sum(pool_exp, axis=1, keepdims=True)
        + jnp.sum(hard_exp, axis=1, keepdims=True)
    )
    target = (positives[:, None] == jnp.arange(rows, dtype=jnp.int32)[None, :]).astype(jnp.float32)
    local_weight = (local_exp / total - target).astype(jnp.bfloat16)
    pool_weight = (pool_exp / total).astype(jnp.bfloat16)
    hard_weight = (hard_exp / total).astype(jnp.bfloat16)
    grad_hard = (SHARPNESS * transposed(hard_weight, queries)).astype(jnp.bfloat16)
    returned = lax.all_to_all(
        grad_hard.reshape(peers, slots * TILE, width), "pb", split_axis=0, concat_axis=0, tiled=True
    ).reshape(hard, width)
    term = SHARPNESS * transposed(pool_weight, queries)
    for bit in reversed(bits):
        half = term.shape[0] // 2
        sent = term[half:]
        if bit not in wide:
            sent = sent.astype(jnp.bfloat16)
        term = term[:half] + exchange(sent, bit, size).astype(jnp.float32)
    grad_pool = term.astype(jnp.bfloat16)
    grad_query = jnp.dot(local_weight, passages, preferred_element_type=jnp.float32)
    grad_query = grad_query + jnp.dot(pool_weight, pooled, preferred_element_type=jnp.float32)
    grad_query = grad_query + jnp.dot(hard_weight, hard_rows, preferred_element_type=jnp.float32)
    grad_queries = (SHARPNESS * grad_query).astype(jnp.bfloat16)
    grad_local = SHARPNESS * transposed(local_weight, queries)
    summed = grad_local + transposed(chosen, returned)
    grad_passages = summed.astype(jnp.bfloat16)
    return (grad_queries, grad_passages, grad_pool)


def solution(mesh):
    bits = (32, 16, 8, 4, 2, 1)
    wide = (1, 8, 16, 32)
    return jax.shard_map(
        lambda *args: body(bits, wide, *args),
        mesh=mesh,
        in_specs=(
            P(("pb", "pool"), None),
            P(("pb", "pool"), None),
            P(("pb", "pool"), None),
            P(("pb", "pool")),
            P("pb", "pool", None, None),
            P("pb", "pool", None),
        ),
        out_specs=(P(("pb", "pool"), None), P(("pb", "pool"), None), P(("pb", "pool"), None)),
        check_vma=False,
    )
```

```python
import jax
import jax.numpy as jnp
from jax import lax
from jax.sharding import PartitionSpec as P

TILE = 8


SHARPNESS = 50.0


def contract(left, right):
    return lax.dot_general(
        left, right, (((1,), (1,)), ((), ())), preferred_element_type=jnp.float32
    )


def transposed(left, right):
    return lax.dot_general(
        left, right, (((0,), (0,)), ((), ())), preferred_element_type=jnp.float32
    )


def shifts(block, step, count, move, sign):
    def moved(j):
        digit = j // step % count
        return j + ((digit + sign * move) % count - digit) * step

    return lax.ppermute(block, "pool", [(j, moved(j)) for j in range(lax.axis_size("pool"))])


def body(digits, queries, passages, pool_passages, positives, tile_ids, tile_count):
    rows, width = queries.shape
    picks = tile_ids[0, 0]
    peers, slots = picks.shape
    hard = peers * slots * TILE
    wanted = (
        picks.reshape(-1)[:, None] * TILE + jnp.arange(TILE, dtype=jnp.int32)[None, :]
    ).reshape(hard)
    chosen = (wanted[:, None] == jnp.arange(rows, dtype=jnp.int32)[None, :]).astype(jnp.bfloat16)
    outgoing = jnp.dot(chosen, passages, preferred_element_type=jnp.float32).astype(jnp.bfloat16)
    hard_rows = lax.all_to_all(
        outgoing.reshape(peers, slots * TILE, width), "pb", split_axis=0, concat_axis=0, tiled=True
    ).reshape(hard, width)
    live = jnp.arange(slots, dtype=jnp.int32)[None, :] < tile_count[0, 0][:, None]
    hard_mask = jnp.broadcast_to(live[:, :, None], (peers, slots, TILE)).reshape(hard)
    pooled = pool_passages
    for step, count, _ in digits:
        pooled = jnp.concatenate(
            [pooled] + [shifts(pooled, step, count, m, -1) for m in range(1, count)], axis=0
        )
    local_logit = SHARPNESS * contract(queries, passages)
    pool_logit = SHARPNESS * contract(queries, pooled)
    hard_logit = jnp.where(hard_mask[None, :], SHARPNESS * contract(queries, hard_rows), -jnp.inf)
    highest = jnp.maximum(
        jnp.max(local_logit, axis=1, keepdims=True), jnp.max(pool_logit, axis=1, keepdims=True)
    )
    highest = jnp.maximum(highest, jnp.max(hard_logit, axis=1, keepdims=True))
    local_exp = jnp.exp(local_logit - highest)
    pool_exp = jnp.exp(pool_logit - highest)
    hard_exp = jnp.exp(hard_logit - highest)
    total = (
        jnp.sum(local_exp, axis=1, keepdims=True)
        + jnp.sum(pool_exp, axis=1, keepdims=True)
        + jnp.sum(hard_exp, axis=1, keepdims=True)
    )
    target = (positives[:, None] == jnp.arange(rows, dtype=jnp.int32)[None, :]).astype(jnp.float32)
    local_weight = (local_exp / total - target).astype(jnp.bfloat16)
    pool_weight = (pool_exp / total).astype(jnp.bfloat16)
    hard_weight = (hard_exp / total).astype(jnp.bfloat16)
    grad_hard = (SHARPNESS * transposed(hard_weight, queries)).astype(jnp.bfloat16)
    returned = lax.all_to_all(
        grad_hard.reshape(peers, slots * TILE, width), "pb", split_axis=0, concat_axis=0, tiled=True
    ).reshape(hard, width)
    term = SHARPNESS * transposed(pool_weight, queries)
    for step, count, link in reversed(digits):
        size = term.shape[0] // count
        pieces = [term[m * size : (m + 1) * size] for m in range(count)]
        term = pieces[0]
        for m in range(1, count):
            term = term + shifts(pieces[m].astype(link), step, count, m, 1).astype(jnp.float32)
    grad_pool = term.astype(jnp.bfloat16)
    grad_query = jnp.dot(local_weight, passages, preferred_element_type=jnp.float32)
    grad_query = grad_query + jnp.dot(pool_weight, pooled, preferred_element_type=jnp.float32)
    grad_query = grad_query + jnp.dot(hard_weight, hard_rows, preferred_element_type=jnp.float32)
    grad_queries = (SHARPNESS * grad_query).astype(jnp.bfloat16)
    grad_local = SHARPNESS * transposed(local_weight, queries)
    summed = grad_local + transposed(chosen, returned)
    grad_passages = summed.astype(jnp.bfloat16)
    return (grad_queries, grad_passages, grad_pool)


def solution(mesh):
    digits = ((8, 8, jnp.float32), (2, 4, jnp.bfloat16), (1, 2, jnp.float32))
    return jax.shard_map(
        lambda *args: body(digits, *args),
        mesh=mesh,
        in_specs=(
            P(("pb", "pool"), None),
            P(("pb", "pool"), None),
            P(("pb", "pool"), None),
            P(("pb", "pool")),
            P("pb", "pool", None, None),
            P("pb", "pool", None),
        ),
        out_specs=(P(("pb", "pool"), None), P(("pb", "pool"), None), P(("pb", "pool"), None)),
        check_vma=False,
    )
```

```python
import functools

import jax
import jax.numpy as jnp
from jax import lax
from jax.experimental import pallas as pl
from jax.experimental.pallas import tpu as pltpu
from jax.sharding import PartitionSpec as P

TILE = 8


SHARPNESS = 50.0

VMEM = pl.BlockSpec(memory_space=pltpu.VMEM)
SMEM = pl.BlockSpec(memory_space=pltpu.SMEM)
ANY = pl.BlockSpec(memory_space=pl.ANY)


def contract(left, right):
    return lax.dot_general(
        left, right, (((1,), (1,)), ((), ())), preferred_element_type=jnp.float32
    )


def transposed(left, right):
    return lax.dot_general(
        left, right, (((0,), (0,)), ((), ())), preferred_element_type=jnp.float32
    )


def shifts(block, step, count, move, sign):
    def moved(j):
        digit = j // step % count
        return j + ((digit + sign * move) % count - digit) * step

    return lax.ppermute(block, "pool", [(j, moved(j)) for j in range(lax.axis_size("pool"))])


def gather_kernel(picks_ref, tiles_ref, out_ref, sems):
    slots, peers = picks_ref.shape
    copies = []
    for peer in range(peers):
        for slot in range(slots):
            j = peer * slots + slot
            copy = pltpu.make_async_copy(
                tiles_ref.at[picks_ref[slot, peer]], out_ref.at[j], sems.at[j]
            )
            copy.start()
            copies.append(copy)
    for copy in copies:
        copy.wait()


def gather_tiles(picks, tiles):
    slots, peers = picks.shape
    return pl.pallas_call(
        gather_kernel,
        out_shape=jax.ShapeDtypeStruct((peers * slots,) + tiles.shape[1:], tiles.dtype),
        in_specs=[SMEM, ANY],
        out_specs=ANY,
        scratch_shapes=[pltpu.SemaphoreType.DMA((peers * slots,))],
        cost_estimate=pl.CostEstimate(flops=0, bytes_accessed=3 << 20, transcendentals=0),
        name="gather_tiles",
    )(picks, tiles)


def scores_kernel(keys_ref, queries_ref, out_ref):
    out_ref[...] = SHARPNESS * contract(keys_ref[...], queries_ref[...])


def scores(keys, queries):
    return pl.pallas_call(
        scores_kernel,
        out_shape=jax.ShapeDtypeStruct((keys.shape[0], queries.shape[0]), jnp.float32),
        in_specs=[VMEM, VMEM],
        out_specs=VMEM,
        cost_estimate=pl.CostEstimate(flops=1 << 20, bytes_accessed=1 << 20, transcendentals=0),
        name="scores",
    )(keys, queries)


def weights_kernel(
    chunk, queries_ref, hard_ref, local_ref, near_ref, far_ref, mask_ref, positives_ref,
    grad_ref, local_out, near_out, far_out, hard_out, buffer, sems,
):
    local, near, far = local_ref[...], near_ref[...], far_ref[...]
    hard = SHARPNESS * contract(hard_ref[...], queries_ref[...])
    hard = jnp.where(mask_ref[...] > 0.0, hard, -jnp.inf)
    top = lambda x: jnp.max(x, axis=0, keepdims=True)
    highest = jnp.maximum(jnp.maximum(top(local), top(near)), jnp.maximum(top(far), top(hard)))
    local, near, far = jnp.exp(local - highest), jnp.exp(near - highest), jnp.exp(far - highest)
    hard = jnp.exp(hard - highest)
    add = lambda x: jnp.sum(x, axis=0, keepdims=True)
    total = add(local) + add(near) + add(far) + add(hard)
    weight = (hard / total).astype(jnp.bfloat16)
    copies = []
    for i in range(queries_ref.shape[1] // chunk):
        columns = pl.ds(i * chunk, chunk)
        part = jnp.dot(weight, queries_ref[:, columns], preferred_element_type=jnp.float32)
        buffer[:, columns] = (SHARPNESS * part).astype(jnp.bfloat16)
        copy = pltpu.make_async_copy(buffer.at[:, columns], grad_ref.at[:, columns], sems.at[i])
        copy.start()
        copies.append(copy)
    hard_out[...] = weight
    rows = lax.broadcasted_iota(jnp.int32, local.shape, 0)
    target = (rows == positives_ref[...]).astype(jnp.float32)
    local_out[...] = (local / total - target).astype(jnp.bfloat16)
    near_out[...] = (near / total).astype(jnp.bfloat16)
    far_out[...] = (far / total).astype(jnp.bfloat16)
    for copy in copies:
        copy.wait()


def weights(queries, hard_rows, local, near, far, mask, positives, chunk=1024):
    hard, width = hard_rows.shape
    like = lambda x: jax.ShapeDtypeStruct(x.shape, jnp.bfloat16)
    return pl.pallas_call(
        functools.partial(weights_kernel, chunk),
        out_shape=(
            jax.ShapeDtypeStruct((hard, width), jnp.bfloat16),
            like(local), like(near), like(far), like(mask),
        ),
        in_specs=[VMEM] * 7,
        out_specs=(ANY, VMEM, VMEM, VMEM, VMEM),
        scratch_shapes=[
            pltpu.VMEM((hard, width), jnp.bfloat16),
            pltpu.SemaphoreType.DMA((width // chunk,)),
        ],
        cost_estimate=pl.CostEstimate(flops=1 << 20, bytes_accessed=1 << 20, transcendentals=0),
        name="weights",
    )(queries, hard_rows, local, near, far, mask, positives)


def pool_kernel(near_ref, far_ref, queries_ref, near_out, far_out):
    near_out[...] = SHARPNESS * jnp.dot(
        near_ref[...], queries_ref[...], preferred_element_type=jnp.float32
    )
    far = SHARPNESS * jnp.dot(far_ref[...], queries_ref[...], preferred_element_type=jnp.float32)
    far_out[...] = far.astype(far_out.dtype)


def pool_terms(near, far, queries, link):
    shape = (near.shape[0], queries.shape[1])
    return pl.pallas_call(
        pool_kernel,
        out_shape=(jax.ShapeDtypeStruct(shape, jnp.float32), jax.ShapeDtypeStruct(shape, link)),
        in_specs=[VMEM] * 3,
        out_specs=(VMEM, VMEM),
        cost_estimate=pl.CostEstimate(flops=1 << 20, bytes_accessed=1 << 20, transcendentals=0),
        name="pool_terms",
    )(near, far, queries)


def queries_kernel(chunk, *refs):
    pairs, (out_ref, buffer, sems) = refs[:-3], refs[-3:]
    count = len(pairs) // 2
    copies = []
    for i in range(out_ref.shape[1] // chunk):
        columns = pl.ds(i * chunk, chunk)
        part = transposed(pairs[0][...], pairs[count][:, columns])
        for k in range(1, count):
            part = part + transposed(pairs[k][...], pairs[count + k][:, columns])
        buffer[:, columns] = (SHARPNESS * part).astype(jnp.bfloat16)
        copy = pltpu.make_async_copy(buffer.at[:, columns], out_ref.at[:, columns], sems.at[i])
        copy.start()
        copies.append(copy)
    for copy in copies:
        copy.wait()


def query_gradient(weight, keys, chunk=1024):
    rows, width = weight[0].shape[1], keys[0].shape[1]
    return pl.pallas_call(
        functools.partial(queries_kernel, chunk),
        out_shape=jax.ShapeDtypeStruct((rows, width), jnp.bfloat16),
        in_specs=[VMEM] * (len(weight) + len(keys)),
        out_specs=ANY,
        scratch_shapes=[
            pltpu.VMEM((rows, width), jnp.bfloat16),
            pltpu.SemaphoreType.DMA((width // chunk,)),
        ],
        cost_estimate=pl.CostEstimate(flops=1 << 20, bytes_accessed=1 << 20, transcendentals=0),
        name="query_gradient",
    )(*weight, *keys)


def passages_kernel(
    chunk, weight_ref, queries_ref, wanted_ref, returned_ref, out_ref, buffer, sems
):
    weight = weight_ref[...]
    rows, hard = weight.shape[0], wanted_ref.shape[1]
    chosen = (
        lax.broadcasted_iota(jnp.int32, (rows, hard), 0) == wanted_ref[...]
    ).astype(jnp.bfloat16)
    copies = []
    for i in range(out_ref.shape[1] // chunk):
        columns = pl.ds(i * chunk, chunk)
        part = SHARPNESS * jnp.dot(
            weight, queries_ref[:, columns], preferred_element_type=jnp.float32
        )
        part = part + jnp.dot(
            chosen, returned_ref[:, columns], preferred_element_type=jnp.float32
        )
        buffer[:, columns] = part.astype(jnp.bfloat16)
        copy = pltpu.make_async_copy(buffer.at[:, columns], out_ref.at[:, columns], sems.at[i])
        copy.start()
        copies.append(copy)
    for copy in copies:
        copy.wait()


def passage_gradient(weight, queries, wanted, returned, chunk=1024):
    rows, width = weight.shape[0], queries.shape[1]
    return pl.pallas_call(
        functools.partial(passages_kernel, chunk),
        out_shape=jax.ShapeDtypeStruct((rows, width), jnp.bfloat16),
        in_specs=[VMEM] * 4,
        out_specs=ANY,
        scratch_shapes=[
            pltpu.VMEM((rows, width), jnp.bfloat16),
            pltpu.SemaphoreType.DMA((width // chunk,)),
        ],
        cost_estimate=pl.CostEstimate(flops=1 << 20, bytes_accessed=1 << 20, transcendentals=0),
        name="passage_gradient",
    )(weight, queries, wanted, returned)


def body(digits, queries, passages, pool_passages, positives, tile_ids, tile_count):
    rows, width = queries.shape
    picks = tile_ids[0, 0]
    peers, slots = picks.shape
    hard = peers * slots * TILE
    outgoing = gather_tiles(picks.T, passages.reshape(rows // TILE, TILE, width))
    hard_rows = lax.all_to_all(
        outgoing.reshape(peers, slots * TILE, width), "pb", split_axis=0, concat_axis=0, tiled=True
    ).reshape(hard, width)
    pooled = pool_passages
    for step, count, _ in digits[:-1]:
        pooled = jnp.concatenate(
            [pooled] + [shifts(pooled, step, count, m, -1) for m in range(1, count)], axis=0
        )
    near = pooled
    last_step, last_count, last_link = digits[-1]
    far = shifts(pooled, last_step, last_count, 1, -1)
    live = jnp.arange(slots, dtype=jnp.int32)[None, :] < tile_count[0, 0][:, None]
    mask = jnp.broadcast_to(live[:, :, None, None], (peers, slots, TILE, rows))
    mask = mask.reshape(hard, rows).astype(jnp.float32)
    grad_hard, local_weight, near_weight, far_weight, hard_weight = weights(
        queries, hard_rows, scores(passages, queries), scores(near, queries), scores(far, queries),
        mask, positives[None, :],
    )
    returned = lax.all_to_all(
        grad_hard.reshape(peers, slots * TILE, width), "pb", split_axis=0, concat_axis=0, tiled=True
    ).reshape(hard, width)
    term, sent = pool_terms(near_weight, far_weight, queries, last_link)
    term = term + shifts(sent, last_step, last_count, 1, 1).astype(jnp.float32)
    for step, count, link in reversed(digits[:-1]):
        size = term.shape[0] // count
        pieces = [term[m * size : (m + 1) * size] for m in range(count)]
        term = pieces[0]
        for m in range(1, count):
            term = term + shifts(pieces[m].astype(link), step, count, m, 1).astype(jnp.float32)
    grad_pool = term.astype(jnp.bfloat16)
    grad_queries = query_gradient(
        (local_weight, near_weight, far_weight, hard_weight), (passages, near, far, hard_rows)
    )
    wanted = (
        picks.reshape(-1)[:, None] * TILE + jnp.arange(TILE, dtype=jnp.int32)[None, :]
    ).reshape(1, hard)
    grad_passages = passage_gradient(local_weight, queries, wanted, returned)
    return (grad_queries, grad_passages, grad_pool)


def solution(mesh):
    digits = ((8, 8, jnp.float32), (2, 4, jnp.bfloat16), (1, 2, jnp.float32))
    return jax.shard_map(
        lambda *args: body(digits, *args),
        mesh=mesh,
        in_specs=(
            P(("pb", "pool"), None),
            P(("pb", "pool"), None),
            P(("pb", "pool"), None),
            P(("pb", "pool")),
            P("pb", "pool", None, None),
            P("pb", "pool", None),
        ),
        out_specs=(P(("pb", "pool"), None), P(("pb", "pool"), None), P(("pb", "pool"), None)),
        check_vma=False,
    )
```

```python
import functools

import jax
import jax.numpy as jnp
from jax import lax
from jax.experimental import pallas as pl
from jax.experimental.pallas import tpu as pltpu
from jax.sharding import PartitionSpec as P

TILE = 8


SHARPNESS = 50.0

VMEM = pl.BlockSpec(memory_space=pltpu.VMEM)
SMEM = pl.BlockSpec(memory_space=pltpu.SMEM)
HBM = pl.BlockSpec(memory_space=pltpu.HBM)
PARAMS = pltpu.CompilerParams(vmem_limit_bytes=8 << 20)
CHEAP = pl.CostEstimate(flops=1 << 20, bytes_accessed=1 << 20, transcendentals=0)


def contract(left, right):
    return lax.dot_general(
        left, right, (((1,), (1,)), ((), ())), preferred_element_type=jnp.float32
    )


def transposed(left, right):
    return lax.dot_general(
        left, right, (((0,), (0,)), ((), ())), preferred_element_type=jnp.float32
    )


def shifts(block, moves, sign):
    def moved(j):
        for step, count, move in moves:
            digit = j // step % count
            j += ((digit + sign * move) % count - digit) * step
        return j

    return lax.ppermute(block, "pool", [(j, moved(j)) for j in range(lax.axis_size("pool"))])


def gather_kernel(picks_ref, tiles_ref, out_ref, buffer, load_sems, store_sems):
    slots, peers = picks_ref.shape
    loads, stores = [], []
    for j in range(peers * slots):
        tile = tiles_ref.at[picks_ref[j % slots, j // slots]]
        loads.append(pltpu.make_async_copy(tile, buffer.at[j], load_sems.at[j]))
        loads[-1].start()
    for j, load in enumerate(loads):
        load.wait()
        stores.append(pltpu.make_async_copy(buffer.at[j], out_ref.at[j], store_sems.at[j]))
        stores[-1].start()
    for store in stores:
        store.wait()


def gather_tiles(picks, tiles):
    slots, peers = picks.shape
    shape = (peers * slots,) + tiles.shape[1:]
    return pl.pallas_call(
        gather_kernel,
        out_shape=pltpu.HBM(shape, tiles.dtype),
        in_specs=[SMEM, HBM],
        out_specs=HBM,
        scratch_shapes=[
            pltpu.VMEM(shape, tiles.dtype),
            pltpu.SemaphoreType.DMA((peers * slots,)),
            pltpu.SemaphoreType.DMA((peers * slots,)),
        ],
        compiler_params=PARAMS,
        cost_estimate=pl.CostEstimate(flops=0, bytes_accessed=3 << 20, transcendentals=0),
        name="gather_tiles",
    )(picks, pltpu.with_memory_space_constraint(tiles, pltpu.HBM))


def scores_kernel(keys_ref, queries_ref, out_ref):
    out_ref[...] = SHARPNESS * contract(keys_ref[...], queries_ref[...])


def scores(keys, queries):
    return pl.pallas_call(
        scores_kernel,
        out_shape=jax.ShapeDtypeStruct((keys.shape[0], queries.shape[0]), jnp.float32),
        in_specs=[VMEM, VMEM],
        out_specs=VMEM,
        compiler_params=PARAMS,
        cost_estimate=CHEAP,
        name="scores",
    )(keys, queries)


def weights_kernel(
    chunk, queries_ref, hard_ref, local_ref, near_ref, far_ref, counts_ref, positives_ref,
    grad_ref, local_out, near_out, far_out, hard_out, buffer, sems,
):
    local, near, far = local_ref[...], near_ref[...], far_ref[...]
    hard = SHARPNESS * contract(hard_ref[...], queries_ref[...])
    peers = counts_ref.shape[1]
    size = hard.shape[0] // peers
    slot = lax.broadcasted_iota(jnp.int32, (size, hard.shape[1]), 0) // TILE
    hard = jnp.concatenate(
        [
            jnp.where(slot < counts_ref[0, i], hard[i * size : (i + 1) * size], -jnp.inf)
            for i in range(peers)
        ],
        axis=0,
    )
    top = lambda x: jnp.max(x, axis=0, keepdims=True)
    highest = jnp.maximum(jnp.maximum(top(local), top(near)), jnp.maximum(top(far), top(hard)))
    local, near, far = jnp.exp(local - highest), jnp.exp(near - highest), jnp.exp(far - highest)
    hard = jnp.exp(hard - highest)
    add = lambda x: jnp.sum(x, axis=0, keepdims=True)
    total = add(local) + add(near) + add(far) + add(hard)
    weight = (hard / total).astype(jnp.bfloat16)
    copies = []
    for i in range(queries_ref.shape[1] // chunk):
        columns = pl.ds(i * chunk, chunk)
        part = jnp.dot(weight, queries_ref[:, columns], preferred_element_type=jnp.float32)
        buffer[:, columns] = (SHARPNESS * part).astype(jnp.bfloat16)
        copy = pltpu.make_async_copy(buffer.at[:, columns], grad_ref.at[:, columns], sems.at[i])
        copy.start()
        copies.append(copy)
    hard_out[...] = weight
    rows = lax.broadcasted_iota(jnp.int32, local.shape, 0)
    target = (rows == positives_ref[...]).astype(jnp.float32)
    local_out[...] = (local / total - target).astype(jnp.bfloat16)
    near_out[...] = (near / total).astype(jnp.bfloat16)
    far_out[...] = (far / total).astype(jnp.bfloat16)
    for copy in copies:
        copy.wait()


def weights(queries, hard_rows, local, near, far, counts, positives, chunk=1024):
    hard, width = hard_rows.shape
    like = lambda x: jax.ShapeDtypeStruct(x.shape, jnp.bfloat16)
    return pl.pallas_call(
        functools.partial(weights_kernel, chunk),
        out_shape=(
            pltpu.HBM((hard, width), jnp.bfloat16),
            like(local), like(near), like(far),
            jax.ShapeDtypeStruct((hard, queries.shape[0]), jnp.bfloat16),
        ),
        in_specs=[VMEM] * 5 + [SMEM, VMEM],
        out_specs=(HBM, VMEM, VMEM, VMEM, VMEM),
        scratch_shapes=[
            pltpu.VMEM((hard, width), jnp.bfloat16),
            pltpu.SemaphoreType.DMA((width // chunk,)),
        ],
        compiler_params=PARAMS,
        cost_estimate=CHEAP,
        name="weights",
    )(queries, hard_rows, local, near, far, counts, positives)


def pool_kernel(near_ref, far_ref, queries_ref, kept_out, *sent_out):
    size = kept_out.shape[0]
    pieces = near_ref.shape[0] // size
    near = jnp.dot(near_ref[...], queries_ref[...], preferred_element_type=jnp.float32)
    kept_out[...] = SHARPNESS * near[:size]
    for m in range(1, pieces):
        piece = SHARPNESS * near[m * size : (m + 1) * size]
        sent_out[m - 1][...] = piece.astype(sent_out[m - 1].dtype)
    far = jnp.dot(far_ref[...], queries_ref[...], preferred_element_type=jnp.float32)
    for m in range(pieces):
        piece = SHARPNESS * far[m * size : (m + 1) * size]
        sent_out[pieces - 1 + m][...] = piece.astype(sent_out[pieces - 1 + m].dtype)


def pool_terms(near, far, queries, size, link):
    shape = (size, queries.shape[1])
    count = 2 * near.shape[0] // size
    return pl.pallas_call(
        pool_kernel,
        out_shape=(jax.ShapeDtypeStruct(shape, jnp.float32),)
        + (jax.ShapeDtypeStruct(shape, link),) * (count - 1),
        in_specs=[VMEM] * 3,
        out_specs=(VMEM,) * count,
        compiler_params=PARAMS,
        cost_estimate=CHEAP,
        name="pool_terms",
    )(near, far, queries)


def queries_kernel(chunk, *refs):
    pairs, (out_ref, buffer, sems) = refs[:-3], refs[-3:]
    count = len(pairs) // 2
    copies = []
    for i in range(out_ref.shape[1] // chunk):
        columns = pl.ds(i * chunk, chunk)
        part = transposed(pairs[0][...], pairs[count][:, columns])
        for k in range(1, count):
            part = part + transposed(pairs[k][...], pairs[count + k][:, columns])
        buffer[:, columns] = (SHARPNESS * part).astype(jnp.bfloat16)
        copy = pltpu.make_async_copy(buffer.at[:, columns], out_ref.at[:, columns], sems.at[i])
        copy.start()
        copies.append(copy)
    for copy in copies:
        copy.wait()


def query_gradient(weight, keys, chunk=1024):
    rows, width = weight[0].shape[1], keys[0].shape[1]
    return pl.pallas_call(
        functools.partial(queries_kernel, chunk),
        out_shape=jax.ShapeDtypeStruct((rows, width), jnp.bfloat16),
        in_specs=[VMEM] * (len(weight) + len(keys)),
        out_specs=HBM,
        scratch_shapes=[
            pltpu.VMEM((rows, width), jnp.bfloat16),
            pltpu.SemaphoreType.DMA((width // chunk,)),
        ],
        compiler_params=PARAMS,
        cost_estimate=CHEAP,
        name="query_gradient",
    )(*weight, *keys)


def passages_kernel(
    chunk, weight_ref, queries_ref, wanted_ref, returned_ref, out_ref,
    incoming, buffer, load_sems, store_sems,
):
    spans = [pl.ds(i * chunk, chunk) for i in range(out_ref.shape[1] // chunk)]
    loads = [
        pltpu.make_async_copy(returned_ref.at[:, span], incoming.at[:, span], load_sems.at[i])
        for i, span in enumerate(spans)
    ]
    for load in loads:
        load.start()
    weight = weight_ref[...]
    rows, hard = weight.shape[0], wanted_ref.shape[1]
    chosen = (
        lax.broadcasted_iota(jnp.int32, (rows, hard), 0) == wanted_ref[...]
    ).astype(jnp.bfloat16)
    stores = []
    for i, span in enumerate(spans):
        part = SHARPNESS * jnp.dot(
            weight, queries_ref[:, span], preferred_element_type=jnp.float32
        )
        loads[i].wait()
        part = part + jnp.dot(chosen, incoming[:, span], preferred_element_type=jnp.float32)
        buffer[:, span] = part.astype(jnp.bfloat16)
        store = pltpu.make_async_copy(buffer.at[:, span], out_ref.at[:, span], store_sems.at[i])
        store.start()
        stores.append(store)
    for store in stores:
        store.wait()


def passage_gradient(weight, queries, wanted, returned, chunk=1024):
    rows, width = weight.shape[0], queries.shape[1]
    return pl.pallas_call(
        functools.partial(passages_kernel, chunk),
        out_shape=jax.ShapeDtypeStruct((rows, width), jnp.bfloat16),
        in_specs=[VMEM] * 3 + [HBM],
        out_specs=HBM,
        scratch_shapes=[
            pltpu.VMEM(returned.shape, jnp.bfloat16),
            pltpu.VMEM((rows, width), jnp.bfloat16),
            pltpu.SemaphoreType.DMA((width // chunk,)),
            pltpu.SemaphoreType.DMA((width // chunk,)),
        ],
        compiler_params=PARAMS,
        cost_estimate=CHEAP,
        name="passage_gradient",
    )(weight, queries, wanted, pltpu.with_memory_space_constraint(returned, pltpu.HBM))


def body(digits, queries, passages, pool_passages, positives, tile_ids, tile_count):
    rows, width = queries.shape
    picks = tile_ids[0, 0]
    peers, slots = picks.shape
    hard = peers * slots * TILE
    outgoing = gather_tiles(picks.T, passages.reshape(rows // TILE, TILE, width))
    hard_rows = lax.all_to_all(
        outgoing.reshape(peers, slots * TILE, width), "pb", split_axis=0, concat_axis=0, tiled=True
    ).reshape(hard, width)
    pooled = pool_passages
    for step, count in digits[:-1]:
        pooled = jnp.concatenate(
            [pooled] + [shifts(pooled, ((step, count, m),), -1) for m in range(1, count)], axis=0
        )
    near = pooled
    far = shifts(near, (digits[-1] + (1,),), -1)
    grad_hard, local_weight, near_weight, far_weight, hard_weight = weights(
        queries, hard_rows, scores(passages, queries), scores(near, queries), scores(far, queries),
        tile_count[0], positives[None, :],
    )
    returned = lax.all_to_all(
        grad_hard.reshape(peers, slots * TILE, width), "pb", split_axis=0, concat_axis=0, tiled=True
    ).reshape(hard, width)
    (y_step, y_count), (x_step, x_count), (core_step, core_count) = digits
    size = y_count * pool_passages.shape[0]
    term, *sent = pool_terms(near_weight, far_weight, queries, size, jnp.bfloat16)
    moves = [(x, core) for core in range(core_count) for x in range(x_count)][1:]
    for piece, (x, core) in zip(sent, moves):
        pair = ((x_step, x_count, x), (core_step, core_count, core))
        term = term + shifts(piece, pair, 1).astype(jnp.float32)
    size = size // y_count
    pieces = [term[m * size : (m + 1) * size] for m in range(y_count)]
    term = pieces[0]
    for m in range(1, y_count):
        term = term + shifts(pieces[m], ((y_step, y_count, m),), 1)
    grad_pool = term.astype(jnp.bfloat16)
    grad_queries = query_gradient(
        (local_weight, near_weight, far_weight, hard_weight), (passages, near, far, hard_rows)
    )
    wanted = (
        picks.reshape(-1)[:, None] * TILE + jnp.arange(TILE, dtype=jnp.int32)[None, :]
    ).reshape(1, hard)
    grad_passages = passage_gradient(local_weight, queries, wanted, returned)
    return (grad_queries, grad_passages, grad_pool)


def solution(mesh):
    digits = ((8, 8), (2, 4), (1, 2))
    return jax.shard_map(
        lambda *args: body(digits, *args),
        mesh=mesh,
        in_specs=(
            P(("pb", "pool"), None),
            P(("pb", "pool"), None),
            P(("pb", "pool"), None),
            P(("pb", "pool")),
            P("pb", "pool", None, None),
            P("pb", "pool", None),
        ),
        out_specs=(P(("pb", "pool"), None), P(("pb", "pool"), None), P(("pb", "pool"), None)),
        check_vma=False,
    )
```

```python
import functools

import jax
import jax.numpy as jnp
from jax import lax
from jax.experimental import pallas as pl
from jax.experimental.pallas import tpu as pltpu
from jax.sharding import PartitionSpec as P

TILE = 8


SHARPNESS = 50.0

VMEM = pl.BlockSpec(memory_space=pltpu.VMEM)
SMEM = pl.BlockSpec(memory_space=pltpu.SMEM)
HBM = pl.BlockSpec(memory_space=pltpu.HBM)
PARAMS = pltpu.CompilerParams(vmem_limit_bytes=8 << 20)
CHEAP = pl.CostEstimate(flops=1 << 20, bytes_accessed=1 << 20, transcendentals=0)


def contract(left, right):
    return lax.dot_general(
        left, right, (((1,), (1,)), ((), ())), preferred_element_type=jnp.float32
    )


def transposed(left, right):
    return lax.dot_general(
        left, right, (((0,), (0,)), ((), ())), preferred_element_type=jnp.float32
    )


def shifts(block, moves, sign):
    def moved(j):
        for step, count, move in moves:
            digit = j // step % count
            j += ((digit + sign * move) % count - digit) * step
        return j

    return lax.ppermute(block, "pool", [(j, moved(j)) for j in range(lax.axis_size("pool"))])


def gather_kernel(parts, picks_ref, tiles_ref, out_ref, buffer, load_sems, store_sems):
    slots, peers = picks_ref.shape
    size = tiles_ref.shape[0] // parts
    loads = []
    for i in range(parts):
        span = pl.ds(i * size, size)
        loads.append(pltpu.make_async_copy(tiles_ref.at[span], buffer.at[span], load_sems.at[i]))
        loads[-1].start()
    for load in loads:
        load.wait()
    stores = []
    for j in range(peers * slots):
        tile = buffer.at[picks_ref[j % slots, j // slots]]
        stores.append(pltpu.make_async_copy(tile, out_ref.at[j], store_sems.at[j]))
        stores[-1].start()
    for store in stores:
        store.wait()


def gather_tiles(picks, tiles, parts=4):
    slots, peers = picks.shape
    shape = (peers * slots,) + tiles.shape[1:]
    return pl.pallas_call(
        functools.partial(gather_kernel, parts),
        out_shape=pltpu.HBM(shape, tiles.dtype),
        in_specs=[SMEM, HBM],
        out_specs=HBM,
        scratch_shapes=[
            pltpu.VMEM(tiles.shape, tiles.dtype),
            pltpu.SemaphoreType.DMA((parts,)),
            pltpu.SemaphoreType.DMA((peers * slots,)),
        ],
        compiler_params=PARAMS,
        cost_estimate=pl.CostEstimate(flops=0, bytes_accessed=3 << 20, transcendentals=0),
        name="gather_tiles",
    )(picks, pltpu.with_memory_space_constraint(tiles, pltpu.HBM))


def scores_kernel(keys_ref, queries_ref, out_ref):
    out_ref[...] = SHARPNESS * contract(keys_ref[...], queries_ref[...])


def scores(keys, queries):
    return pl.pallas_call(
        scores_kernel,
        out_shape=jax.ShapeDtypeStruct((keys.shape[0], queries.shape[0]), jnp.float32),
        in_specs=[VMEM, VMEM],
        out_specs=VMEM,
        compiler_params=PARAMS,
        cost_estimate=CHEAP,
        name="scores",
    )(keys, queries)


def weights_kernel(
    chunk, queries_ref, hard_ref, local_ref, near_ref, far_ref, counts_ref, positives_ref,
    grad_ref, local_out, near_out, far_out, hard_out, buffer, sems,
):
    local, near, far = local_ref[...], near_ref[...], far_ref[...]
    hard = SHARPNESS * contract(hard_ref[...], queries_ref[...])
    peers = counts_ref.shape[1]
    size = hard.shape[0] // peers
    slot = lax.broadcasted_iota(jnp.int32, (size, hard.shape[1]), 0) // TILE
    hard = jnp.concatenate(
        [
            jnp.where(slot < counts_ref[0, i], hard[i * size : (i + 1) * size], -jnp.inf)
            for i in range(peers)
        ],
        axis=0,
    )
    top = lambda x: jnp.max(x, axis=0, keepdims=True)
    highest = jnp.maximum(jnp.maximum(top(local), top(near)), jnp.maximum(top(far), top(hard)))
    local, near, far = jnp.exp(local - highest), jnp.exp(near - highest), jnp.exp(far - highest)
    hard = jnp.exp(hard - highest)
    add = lambda x: jnp.sum(x, axis=0, keepdims=True)
    total = add(local) + add(near) + add(far) + add(hard)
    weight = (hard / total).astype(jnp.bfloat16)
    copies = []
    for i in range(queries_ref.shape[1] // chunk):
        columns = pl.ds(i * chunk, chunk)
        part = jnp.dot(weight, queries_ref[:, columns], preferred_element_type=jnp.float32)
        buffer[:, columns] = (SHARPNESS * part).astype(jnp.bfloat16)
        copy = pltpu.make_async_copy(buffer.at[:, columns], grad_ref.at[:, columns], sems.at[i])
        copy.start()
        copies.append(copy)
    hard_out[...] = weight
    rows = lax.broadcasted_iota(jnp.int32, local.shape, 0)
    target = (rows == positives_ref[...]).astype(jnp.float32)
    local_out[...] = (local / total - target).astype(jnp.bfloat16)
    near_out[...] = (near / total).astype(jnp.bfloat16)
    far_out[...] = (far / total).astype(jnp.bfloat16)
    for copy in copies:
        copy.wait()


def weights(queries, hard_rows, local, near, far, counts, positives, chunk=512):
    hard, width = hard_rows.shape
    like = lambda x: jax.ShapeDtypeStruct(x.shape, jnp.bfloat16)
    return pl.pallas_call(
        functools.partial(weights_kernel, chunk),
        out_shape=(
            pltpu.HBM((hard, width), jnp.bfloat16),
            like(local), like(near), like(far),
            jax.ShapeDtypeStruct((hard, queries.shape[0]), jnp.bfloat16),
        ),
        in_specs=[VMEM] * 5 + [SMEM, VMEM],
        out_specs=(HBM, VMEM, VMEM, VMEM, VMEM),
        scratch_shapes=[
            pltpu.VMEM((hard, width), jnp.bfloat16),
            pltpu.SemaphoreType.DMA((width // chunk,)),
        ],
        compiler_params=PARAMS,
        cost_estimate=CHEAP,
        name="weights",
    )(queries, hard_rows, local, near, far, counts, positives)


def pool_kernel(near_ref, far_ref, queries_ref, kept_out, *sent_out):
    size = kept_out.shape[0]
    pieces = near_ref.shape[0] // size
    near = jnp.dot(near_ref[...], queries_ref[...], preferred_element_type=jnp.float32)
    kept_out[...] = SHARPNESS * near[:size]
    for m in range(1, pieces):
        piece = SHARPNESS * near[m * size : (m + 1) * size]
        sent_out[m - 1][...] = piece.astype(sent_out[m - 1].dtype)
    far = jnp.dot(far_ref[...], queries_ref[...], preferred_element_type=jnp.float32)
    for m in range(pieces):
        piece = SHARPNESS * far[m * size : (m + 1) * size]
        sent_out[pieces - 1 + m][...] = piece.astype(sent_out[pieces - 1 + m].dtype)


def pool_terms(near, far, queries, size, link):
    shape = (size, queries.shape[1])
    count = 2 * near.shape[0] // size
    return pl.pallas_call(
        pool_kernel,
        out_shape=(jax.ShapeDtypeStruct(shape, jnp.float32),)
        + (jax.ShapeDtypeStruct(shape, link),) * (count - 1),
        in_specs=[VMEM] * 3,
        out_specs=(VMEM,) * count,
        compiler_params=PARAMS,
        cost_estimate=CHEAP,
        name="pool_terms",
    )(near, far, queries)


def queries_kernel(chunk, weight_refs, picks_ref, hard_ref, key_refs, outs, scratch):
    out_ref, chosen_ref = outs
    held, buffer, load_sems, store_sems = scratch
    spans = [pl.ds(i * chunk, chunk) for i in range(out_ref.shape[1] // chunk)]
    loads, views, start = [], [], 0
    for k, key in enumerate(key_refs):
        view = held.at[pl.ds(start, key.shape[0])]
        start += key.shape[0]
        views.append(view)
        loads.append(
            [
                pltpu.make_async_copy(key.at[:, span], view.at[:, span], load_sems.at[k, i])
                for i, span in enumerate(spans)
            ]
        )
    for i in range(len(spans)):
        for load in loads:
            load[i].start()
    slots, peers = picks_ref.shape
    lane = lax.broadcasted_iota(jnp.int32, (1, chosen_ref.shape[1]), 1)
    wanted = lane % TILE
    for j in range(peers * slots):
        pick = picks_ref[j % slots, j // slots]
        wanted = wanted + jnp.where(lane // TILE == j, pick * TILE, 0)
    rows = lax.broadcasted_iota(jnp.int32, chosen_ref.shape, 0)
    chosen_ref[...] = (rows == wanted).astype(jnp.float32).astype(jnp.bfloat16)
    hard_weight, weight = weight_refs[0][...], [ref[...] for ref in weight_refs[1:]]
    stores = []
    for i, span in enumerate(spans):
        part = transposed(hard_weight, hard_ref[:, span])
        for k, view in enumerate(views):
            loads[k][i].wait()
            part = part + transposed(weight[k], view[:, span])
        buffer[:, span] = (SHARPNESS * part).astype(jnp.bfloat16)
        store = pltpu.make_async_copy(buffer.at[:, span], out_ref.at[:, span], store_sems.at[i])
        store.start()
        stores.append(store)
    for store in stores:
        store.wait()


def query_gradient(hard_weight, weight, picks, hard_rows, keys, chunk=1024):
    (hard, rows), width = hard_weight.shape, hard_rows.shape[1]
    held = sum(key.shape[0] for key in keys)
    count = len(keys)

    def kernel(*refs):
        inputs, outs, scratch = refs[: 3 + 2 * count], refs[3 + 2 * count : 5 + 2 * count], refs[5 + 2 * count :]
        queries_kernel(
            chunk, inputs[: 1 + count], inputs[1 + count], inputs[2 + count],
            inputs[3 + count :], outs, scratch,
        )

    return pl.pallas_call(
        kernel,
        out_shape=(
            pltpu.HBM((rows, width), jnp.bfloat16),
            jax.ShapeDtypeStruct((rows, hard), jnp.bfloat16),
        ),
        in_specs=[VMEM] * (1 + count) + [SMEM, VMEM] + [HBM] * count,
        out_specs=(HBM, VMEM),
        scratch_shapes=[
            pltpu.VMEM((held, width), jnp.bfloat16),
            pltpu.VMEM((rows, width), jnp.bfloat16),
            pltpu.SemaphoreType.DMA((count, width // chunk)),
            pltpu.SemaphoreType.DMA((width // chunk,)),
        ],
        compiler_params=PARAMS,
        cost_estimate=CHEAP,
        name="query_gradient",
    )(
        hard_weight, *weight, picks, hard_rows,
        *[pltpu.with_memory_space_constraint(key, pltpu.HBM) for key in keys],
    )


def passages_kernel(
    chunk, weight_ref, queries_ref, chosen_ref, returned_ref, out_ref,
    incoming, buffer, load_sems, store_sems,
):
    spans = [pl.ds(i * chunk, chunk) for i in range(out_ref.shape[1] // chunk)]
    loads = [
        pltpu.make_async_copy(returned_ref.at[:, span], incoming.at[:, span], load_sems.at[i])
        for i, span in enumerate(spans)
    ]
    for load in loads:
        load.start()
    weight = weight_ref[...]
    chosen = chosen_ref[...]
    stores = []
    for i, span in enumerate(spans):
        part = SHARPNESS * jnp.dot(
            weight, queries_ref[:, span], preferred_element_type=jnp.float32
        )
        loads[i].wait()
        part = part + jnp.dot(chosen, incoming[:, span], preferred_element_type=jnp.float32)
        buffer[:, span] = part.astype(jnp.bfloat16)
        store = pltpu.make_async_copy(buffer.at[:, span], out_ref.at[:, span], store_sems.at[i])
        store.start()
        stores.append(store)
    for store in stores:
        store.wait()


def passage_gradient(weight, queries, chosen, returned, chunk=1024):
    rows, width = weight.shape[0], queries.shape[1]
    return pl.pallas_call(
        functools.partial(passages_kernel, chunk),
        out_shape=jax.ShapeDtypeStruct((rows, width), jnp.bfloat16),
        in_specs=[VMEM] * 3 + [HBM],
        out_specs=HBM,
        scratch_shapes=[
            pltpu.VMEM(returned.shape, jnp.bfloat16),
            pltpu.VMEM((rows, width), jnp.bfloat16),
            pltpu.SemaphoreType.DMA((width // chunk,)),
            pltpu.SemaphoreType.DMA((width // chunk,)),
        ],
        compiler_params=PARAMS,
        cost_estimate=CHEAP,
        name="passage_gradient",
    )(weight, queries, chosen, pltpu.with_memory_space_constraint(returned, pltpu.HBM))


def body(digits, queries, passages, pool_passages, positives, tile_ids, tile_count):
    rows, width = queries.shape
    picks = tile_ids[0, 0]
    peers, slots = picks.shape
    hard = peers * slots * TILE
    outgoing = gather_tiles(picks.T, passages.reshape(rows // TILE, TILE, width))
    hard_rows = lax.all_to_all(
        outgoing.reshape(peers, slots * TILE, width), "pb", split_axis=0, concat_axis=0, tiled=True
    ).reshape(hard, width)
    pooled = pool_passages
    for step, count in digits[:-1]:
        pooled = jnp.concatenate(
            [pooled] + [shifts(pooled, ((step, count, m),), -1) for m in range(1, count)], axis=0
        )
    near = pooled
    far = shifts(near, (digits[-1] + (1,),), -1)
    grad_hard, local_weight, near_weight, far_weight, hard_weight = weights(
        queries, hard_rows, scores(passages, queries), scores(near, queries), scores(far, queries),
        tile_count[0], positives[None, :],
    )
    returned = lax.all_to_all(
        grad_hard.reshape(peers, slots * TILE, width), "pb", split_axis=0, concat_axis=0, tiled=True
    ).reshape(hard, width)
    *y_digits, (x_step, x_count), (core_step, core_count) = digits
    size = pooled.shape[0] // x_count
    term, *sent = pool_terms(near_weight, far_weight, queries, size, jnp.bfloat16)
    moves = [(x, core) for core in range(core_count) for x in range(x_count)][1:]
    for piece, (x, core) in zip(sent, moves):
        pair = ((x_step, x_count, x), (core_step, core_count, core))
        term = term + shifts(piece, pair, 1).astype(jnp.float32)
    for step, count in reversed(y_digits):
        size = size // count
        pieces = [term[m * size : (m + 1) * size] for m in range(count)]
        term = pieces[0]
        for m in range(1, count):
            term = term + shifts(pieces[m], ((step, count, m),), 1)
    grad_pool = term.astype(jnp.bfloat16)
    grad_queries, chosen = query_gradient(
        hard_weight, (local_weight, near_weight, far_weight), picks.T, hard_rows,
        (passages, near, far),
    )
    grad_passages = passage_gradient(local_weight, queries, chosen, returned)
    return (grad_queries, grad_passages, grad_pool)


def solution(mesh):
    digits = ((8, 4), (32, 2), (2, 4), (1, 2))
    return jax.shard_map(
        lambda *args: body(digits, *args),
        mesh=mesh,
        in_specs=(
            P(("pb", "pool"), None),
            P(("pb", "pool"), None),
            P(("pb", "pool"), None),
            P(("pb", "pool")),
            P("pb", "pool", None, None),
            P("pb", "pool", None),
        ),
        out_specs=(P(("pb", "pool"), None), P(("pb", "pool"), None), P(("pb", "pool"), None)),
        check_vma=False,
    )
```

```python
import functools

import jax
import jax.numpy as jnp
from jax import lax
from jax.experimental import pallas as pl
from jax.experimental.pallas import tpu as pltpu
from jax.sharding import PartitionSpec as P

TILE = 8

ORDERS = ((0, 3, 6, 9, 1, 4, 7, 10, 2, 5, 8, 11), (6, 9, 0, 3, 7, 10, 1, 8, 4, 11, 2, 5))

SHARPNESS = 50.0

VMEM = pl.BlockSpec(memory_space=pltpu.VMEM)
SMEM = pl.BlockSpec(memory_space=pltpu.SMEM)
HBM = pl.BlockSpec(memory_space=pltpu.HBM)
PARAMS = pltpu.CompilerParams(vmem_limit_bytes=8 << 20)
CHEAP = pl.CostEstimate(flops=1 << 20, bytes_accessed=1 << 20, transcendentals=0)


def contract(left, right):
    return lax.dot_general(
        left, right, (((1,), (1,)), ((), ())), preferred_element_type=jnp.float32
    )


def transposed(left, right):
    return lax.dot_general(
        left, right, (((0,), (0,)), ((), ())), preferred_element_type=jnp.float32
    )


def member(k):
    first, second = ORDERS[0][k], ORDERS[1][k]
    return first + lax.axis_index("pool") % 2 * (second - first)


def trade(blocks):
    size = lax.axis_size("pool")
    groups = [[z * size + p for z in ORDERS[p % 2]] for p in range(size)]
    return lax.all_to_all(
        blocks, ("pb", "pool"), split_axis=0, concat_axis=0, tiled=True, axis_index_groups=groups
    )


def shifts(block, moves, sign):
    def moved(j):
        for step, count, move in moves:
            digit = j // step % count
            j += ((digit + sign * move) % count - digit) * step
        return j

    return lax.ppermute(block, "pool", [(j, moved(j)) for j in range(lax.axis_size("pool"))])


def gather_kernel(parts, picks_ref, tiles_ref, out_ref, buffer, load_sems, store_sems):
    slots, peers = picks_ref.shape
    size = tiles_ref.shape[0] // parts
    loads = []
    for i in range(parts):
        span = pl.ds(i * size, size)
        loads.append(pltpu.make_async_copy(tiles_ref.at[span], buffer.at[span], load_sems.at[i]))
        loads[-1].start()
    for load in loads:
        load.wait()
    stores = []
    for j in range(peers * slots):
        tile = buffer.at[picks_ref[j % slots, member(j // slots)]]
        stores.append(pltpu.make_async_copy(tile, out_ref.at[j], store_sems.at[j]))
        stores[-1].start()
    for store in stores:
        store.wait()


def gather_tiles(picks, tiles, parts=4):
    slots, peers = picks.shape
    shape = (peers * slots,) + tiles.shape[1:]
    return pl.pallas_call(
        functools.partial(gather_kernel, parts),
        out_shape=pltpu.HBM(shape, tiles.dtype),
        in_specs=[SMEM, HBM],
        out_specs=HBM,
        scratch_shapes=[
            pltpu.VMEM(tiles.shape, tiles.dtype),
            pltpu.SemaphoreType.DMA((parts,)),
            pltpu.SemaphoreType.DMA((peers * slots,)),
        ],
        compiler_params=PARAMS,
        cost_estimate=pl.CostEstimate(flops=0, bytes_accessed=3 << 20, transcendentals=0),
        name="gather_tiles",
    )(picks, pltpu.with_memory_space_constraint(tiles, pltpu.HBM))


def scores_kernel(keys_ref, queries_ref, out_ref):
    out_ref[...] = SHARPNESS * contract(keys_ref[...], queries_ref[...])


def scores(keys, queries):
    return pl.pallas_call(
        scores_kernel,
        out_shape=jax.ShapeDtypeStruct((keys.shape[0], queries.shape[0]), jnp.float32),
        in_specs=[VMEM, VMEM],
        out_specs=VMEM,
        compiler_params=PARAMS,
        cost_estimate=CHEAP,
        name="scores",
    )(keys, queries)


def local_kernel(keys_ref, queries_ref, picks_ref, out_ref, chosen_ref):
    out_ref[...] = SHARPNESS * contract(keys_ref[...], queries_ref[...])
    slots, peers = picks_ref.shape
    lane = lax.broadcasted_iota(jnp.int32, (1, chosen_ref.shape[1]), 1)
    wanted = lane % TILE
    for j in range(peers * slots):
        pick = picks_ref[j % slots, member(j // slots)]
        wanted = wanted + jnp.where(lane // TILE == j, pick * TILE, 0)
    rows = lax.broadcasted_iota(jnp.int32, chosen_ref.shape, 0)
    chosen_ref[...] = (rows == wanted).astype(jnp.float32).astype(jnp.bfloat16)


def local_scores(keys, queries, picks):
    rows, hard = keys.shape[0], picks.size * TILE
    return pl.pallas_call(
        local_kernel,
        out_shape=(
            jax.ShapeDtypeStruct((rows, queries.shape[0]), jnp.float32),
            jax.ShapeDtypeStruct((rows, hard), jnp.bfloat16),
        ),
        in_specs=[VMEM, VMEM, SMEM],
        out_specs=(VMEM, VMEM),
        compiler_params=PARAMS,
        cost_estimate=CHEAP,
        name="local_scores",
    )(keys, queries, picks)


def weights_kernel(
    chunk, queries_ref, hard_ref, local_ref, near_ref, far_ref, counts_ref, positives_ref,
    grad_ref, local_out, near_out, far_out, hard_out, buffer, sems,
):
    local, near, far = local_ref[...], near_ref[...], far_ref[...]
    hard = SHARPNESS * contract(hard_ref[...], queries_ref[...])
    peers = counts_ref.shape[1]
    size = hard.shape[0] // peers
    slot = lax.broadcasted_iota(jnp.int32, (size, hard.shape[1]), 0) // TILE
    hard = jnp.concatenate(
        [
            jnp.where(slot < counts_ref[0, member(i)], hard[i * size : (i + 1) * size], -jnp.inf)
            for i in range(peers)
        ],
        axis=0,
    )
    top = lambda x: jnp.max(x, axis=0, keepdims=True)
    highest = jnp.maximum(jnp.maximum(top(local), top(near)), jnp.maximum(top(far), top(hard)))
    local, near, far = jnp.exp(local - highest), jnp.exp(near - highest), jnp.exp(far - highest)
    hard = jnp.exp(hard - highest)
    add = lambda x: jnp.sum(x, axis=0, keepdims=True)
    total = add(local) + add(near) + add(far) + add(hard)
    weight = (hard / total).astype(jnp.bfloat16)
    copies = []
    for i in range(queries_ref.shape[1] // chunk):
        columns = pl.ds(i * chunk, chunk)
        part = jnp.dot(weight, queries_ref[:, columns], preferred_element_type=jnp.float32)
        buffer[:, columns] = (SHARPNESS * part).astype(jnp.bfloat16)
        copy = pltpu.make_async_copy(buffer.at[:, columns], grad_ref.at[:, columns], sems.at[i])
        copy.start()
        copies.append(copy)
    hard_out[...] = weight
    rows = lax.broadcasted_iota(jnp.int32, local.shape, 0)
    target = (rows == positives_ref[...]).astype(jnp.float32)
    local_out[...] = (local / total - target).astype(jnp.bfloat16)
    near_out[...] = (near / total).astype(jnp.bfloat16)
    far_out[...] = (far / total).astype(jnp.bfloat16)
    for copy in copies:
        copy.wait()


def weights(queries, hard_rows, local, near, far, counts, positives, chunk=512):
    hard, width = hard_rows.shape
    like = lambda x: jax.ShapeDtypeStruct(x.shape, jnp.bfloat16)
    return pl.pallas_call(
        functools.partial(weights_kernel, chunk),
        out_shape=(
            pltpu.HBM((hard, width), jnp.bfloat16),
            like(local), like(near), like(far),
            jax.ShapeDtypeStruct((hard, queries.shape[0]), jnp.bfloat16),
        ),
        in_specs=[VMEM] * 5 + [SMEM, VMEM],
        out_specs=(HBM, VMEM, VMEM, VMEM, VMEM),
        scratch_shapes=[
            pltpu.VMEM((hard, width), jnp.bfloat16),
            pltpu.SemaphoreType.DMA((width // chunk,)),
        ],
        compiler_params=PARAMS,
        cost_estimate=CHEAP,
        name="weights",
    )(queries, hard_rows, local, near, far, counts, positives)


def pool_kernel(near_ref, far_ref, queries_ref, kept_out, *sent_out):
    size = kept_out.shape[0]
    pieces = near_ref.shape[0] // size
    near = jnp.dot(near_ref[...], queries_ref[...], preferred_element_type=jnp.float32)
    kept_out[...] = SHARPNESS * near[:size]
    for m in range(1, pieces):
        piece = SHARPNESS * near[m * size : (m + 1) * size]
        sent_out[m - 1][...] = piece.astype(sent_out[m - 1].dtype)
    far = jnp.dot(far_ref[...], queries_ref[...], preferred_element_type=jnp.float32)
    for m in range(pieces):
        piece = SHARPNESS * far[m * size : (m + 1) * size]
        sent_out[pieces - 1 + m][...] = piece.astype(sent_out[pieces - 1 + m].dtype)


def pool_terms(near, far, queries, size, link):
    shape = (size, queries.shape[1])
    count = 2 * near.shape[0] // size
    return pl.pallas_call(
        pool_kernel,
        out_shape=(jax.ShapeDtypeStruct(shape, jnp.float32),)
        + (jax.ShapeDtypeStruct(shape, link),) * (count - 1),
        in_specs=[VMEM] * 3,
        out_specs=(VMEM,) * count,
        compiler_params=PARAMS,
        cost_estimate=CHEAP,
        name="pool_terms",
    )(near, far, queries)


def queries_kernel(
    chunk, hard_weight_ref, local_ref, near_ref, far_ref, hard_ref, passages_ref, pool_near_ref,
    pool_far_ref, out_ref, held, buffer, load_sems, store_sems,
):
    spans = [pl.ds(i * chunk, chunk) for i in range(out_ref.shape[1] // chunk)]
    loads, start = [], 0
    for k, key in enumerate((passages_ref, pool_near_ref, pool_far_ref)):
        view = held.at[pl.ds(start, key.shape[0])]
        start += key.shape[0]
        loads.append(
            [
                pltpu.make_async_copy(key.at[:, span], view.at[:, span], load_sems.at[k, i])
                for i, span in enumerate(spans)
            ]
        )
    for i in range(len(spans)):
        for load in loads:
            load[i].start()
    turned = lambda x: x.astype(jnp.float32).T.astype(jnp.bfloat16)
    hard_weight = turned(hard_weight_ref[...])
    weight = turned(jnp.concatenate([local_ref[...], near_ref[...], far_ref[...]], axis=0))
    stores = []
    for i, span in enumerate(spans):
        part = jnp.dot(hard_weight, hard_ref[:, span], preferred_element_type=jnp.float32)
        for load in loads:
            load[i].wait()
        part = part + jnp.dot(weight, held[:, span], preferred_element_type=jnp.float32)
        buffer[:, span] = (SHARPNESS * part).astype(jnp.bfloat16)
        store = pltpu.make_async_copy(buffer.at[:, span], out_ref.at[:, span], store_sems.at[i])
        store.start()
        stores.append(store)
    for store in stores:
        store.wait()


def query_gradient(hard_weight, weight, hard_rows, keys, chunk=1024):
    rows, width = hard_weight.shape[1], hard_rows.shape[1]
    return pl.pallas_call(
        functools.partial(queries_kernel, chunk),
        out_shape=pltpu.HBM((rows, width), jnp.bfloat16),
        in_specs=[VMEM] * 5 + [HBM] * 3,
        out_specs=HBM,
        scratch_shapes=[
            pltpu.VMEM((sum(key.shape[0] for key in keys), width), jnp.bfloat16),
            pltpu.VMEM((rows, width), jnp.bfloat16),
            pltpu.SemaphoreType.DMA((len(keys), width // chunk)),
            pltpu.SemaphoreType.DMA((width // chunk,)),
        ],
        compiler_params=PARAMS,
        cost_estimate=CHEAP,
        name="query_gradient",
    )(
        hard_weight, *weight, hard_rows,
        *[pltpu.with_memory_space_constraint(key, pltpu.HBM) for key in keys],
    )


def passages_kernel(
    chunk, weight_ref, queries_ref, chosen_ref, returned_ref, out_ref,
    incoming, buffer, load_sems, store_sems,
):
    spans = [pl.ds(i * chunk, chunk) for i in range(out_ref.shape[1] // chunk)]
    loads = [
        pltpu.make_async_copy(returned_ref.at[:, span], incoming.at[:, span], load_sems.at[i])
        for i, span in enumerate(spans)
    ]
    for load in loads:
        load.start()
    weight = weight_ref[...]
    chosen = chosen_ref[...]
    stores = []
    for i, span in enumerate(spans):
        part = SHARPNESS * jnp.dot(
            weight, queries_ref[:, span], preferred_element_type=jnp.float32
        )
        loads[i].wait()
        part = part + jnp.dot(chosen, incoming[:, span], preferred_element_type=jnp.float32)
        buffer[:, span] = part.astype(jnp.bfloat16)
        store = pltpu.make_async_copy(buffer.at[:, span], out_ref.at[:, span], store_sems.at[i])
        store.start()
        stores.append(store)
    for store in stores:
        store.wait()


def passage_gradient(weight, queries, chosen, returned, chunk=1024):
    rows, width = weight.shape[0], queries.shape[1]
    return pl.pallas_call(
        functools.partial(passages_kernel, chunk),
        out_shape=jax.ShapeDtypeStruct((rows, width), jnp.bfloat16),
        in_specs=[VMEM] * 3 + [HBM],
        out_specs=HBM,
        scratch_shapes=[
            pltpu.VMEM(returned.shape, jnp.bfloat16),
            pltpu.VMEM((rows, width), jnp.bfloat16),
            pltpu.SemaphoreType.DMA((width // chunk,)),
            pltpu.SemaphoreType.DMA((width // chunk,)),
        ],
        compiler_params=PARAMS,
        cost_estimate=CHEAP,
        name="passage_gradient",
    )(weight, queries, chosen, pltpu.with_memory_space_constraint(returned, pltpu.HBM))


def body(digits, queries, passages, pool_passages, positives, tile_ids, tile_count):
    rows, width = queries.shape
    picks = tile_ids[0, 0]
    peers, slots = picks.shape
    hard = peers * slots * TILE
    outgoing = gather_tiles(picks.T, passages.reshape(rows // TILE, TILE, width))
    hard_rows = trade(outgoing.reshape(peers, slots * TILE, width)).reshape(hard, width)
    pooled = pool_passages
    for step, count in digits[:-1]:
        pooled = jnp.concatenate(
            [pooled] + [shifts(pooled, ((step, count, m),), -1) for m in range(1, count)], axis=0
        )
    near = pooled
    far = shifts(near, (digits[-1] + (1,),), -1)
    local, chosen = local_scores(passages, queries, picks.T)
    grad_hard, local_weight, near_weight, far_weight, hard_weight = weights(
        queries, hard_rows, local, scores(near, queries), scores(far, queries),
        tile_count[0], positives[None, :],
    )
    returned = trade(grad_hard.reshape(peers, slots * TILE, width)).reshape(hard, width)
    *y_digits, (x_step, x_count), (core_step, core_count) = digits
    size = pooled.shape[0] // x_count
    term, *sent = pool_terms(near_weight, far_weight, queries, size, jnp.bfloat16)
    moves = [(x, core) for core in range(core_count) for x in range(x_count)][1:]
    for piece, (x, core) in zip(sent, moves):
        pair = ((x_step, x_count, x), (core_step, core_count, core))
        term = term + shifts(piece, pair, 1).astype(jnp.float32)
    for step, count in reversed(y_digits):
        size = size // count
        pieces = [term[m * size : (m + 1) * size] for m in range(count)]
        term = pieces[0]
        for m in range(1, count):
            term = term + shifts(pieces[m], ((step, count, m),), 1)
    grad_pool = term.astype(jnp.bfloat16)
    grad_queries = query_gradient(
        hard_weight, (local_weight, near_weight, far_weight), hard_rows, (passages, near, far)
    )
    grad_passages = passage_gradient(local_weight, queries, chosen, returned)
    return (grad_queries, grad_passages, grad_pool)


def solution(mesh):
    digits = ((8, 4), (32, 2), (2, 4), (1, 2))
    return jax.shard_map(
        lambda *args: body(digits, *args),
        mesh=mesh,
        in_specs=(
            P(("pb", "pool"), None),
            P(("pb", "pool"), None),
            P(("pb", "pool"), None),
            P(("pb", "pool")),
            P("pb", "pool", None, None),
            P("pb", "pool", None),
        ),
        out_specs=(P(("pb", "pool"), None), P(("pb", "pool"), None), P(("pb", "pool"), None)),
        check_vma=False,
    )
```

```python
import functools

import jax
import jax.numpy as jnp
from jax import lax
from jax.experimental import pallas as pl
from jax.experimental.pallas import tpu as pltpu
from jax.sharding import PartitionSpec as P

TILE = 8

ORDERS = ((0, 3, 6, 9, 1, 4, 7, 10, 2, 5, 8, 11), (6, 9, 0, 3, 7, 10, 1, 8, 4, 11, 2, 5))

SHARPNESS = 50.0

VMEM = pl.BlockSpec(memory_space=pltpu.VMEM)
SMEM = pl.BlockSpec(memory_space=pltpu.SMEM)
HBM = pl.BlockSpec(memory_space=pltpu.HBM)
PARAMS = pltpu.CompilerParams(vmem_limit_bytes=8 << 20)
CHEAP = pl.CostEstimate(flops=1 << 20, bytes_accessed=1 << 20, transcendentals=0)


def contract(left, right):
    return lax.dot_general(
        left, right, (((1,), (1,)), ((), ())), preferred_element_type=jnp.float32
    )


def transposed(left, right):
    return lax.dot_general(
        left, right, (((0,), (0,)), ((), ())), preferred_element_type=jnp.float32
    )


def member(k):
    first, second = ORDERS[0][k], ORDERS[1][k]
    return first + lax.axis_index("pool") % 2 * (second - first)


def trade(blocks):
    size = lax.axis_size("pool")
    groups = [[z * size + p for z in ORDERS[p % 2]] for p in range(size)]
    return lax.all_to_all(
        blocks, ("pb", "pool"), split_axis=0, concat_axis=0, tiled=True, axis_index_groups=groups
    )


def shifts(block, moves, sign):
    def moved(j):
        for step, count, move in moves:
            digit = j // step % count
            j += ((digit + sign * move) % count - digit) * step
        return j

    return lax.ppermute(block, "pool", [(j, moved(j)) for j in range(lax.axis_size("pool"))])


def gather_kernel(
    parts, picks_ref, tiles_ref, out_ref, picks, buffer, picks_sem, load_sems, store_sems
):
    read = pltpu.make_async_copy(picks_ref, picks, picks_sem)
    read.start()
    size = tiles_ref.shape[0] // parts
    loads = []
    for i in range(parts):
        span = pl.ds(i * size, size)
        loads.append(pltpu.make_async_copy(tiles_ref.at[span], buffer.at[span], load_sems.at[i]))
        loads[-1].start()
    read.wait()
    for load in loads:
        load.wait()
    slots, peers = picks_ref.shape
    stores = []
    for j in range(peers * slots):
        tile = buffer.at[picks[j % slots, member(j // slots)]]
        stores.append(pltpu.make_async_copy(tile, out_ref.at[j], store_sems.at[j]))
        stores[-1].start()
    for store in stores:
        store.wait()


def gather_tiles(picks, tiles, parts=4):
    slots, peers = picks.shape
    shape = (peers * slots,) + tiles.shape[1:]
    return pl.pallas_call(
        functools.partial(gather_kernel, parts),
        out_shape=pltpu.HBM(shape, tiles.dtype),
        in_specs=[HBM, HBM],
        out_specs=HBM,
        scratch_shapes=[
            pltpu.SMEM(picks.shape, picks.dtype),
            pltpu.VMEM(tiles.shape, tiles.dtype),
            pltpu.SemaphoreType.DMA,
            pltpu.SemaphoreType.DMA((parts,)),
            pltpu.SemaphoreType.DMA((peers * slots,)),
        ],
        compiler_params=PARAMS,
        cost_estimate=pl.CostEstimate(flops=0, bytes_accessed=3 << 20, transcendentals=0),
        name="gather_tiles",
    )(
        pltpu.with_memory_space_constraint(picks, pltpu.HBM),
        pltpu.with_memory_space_constraint(tiles, pltpu.HBM),
    )


def scores_kernel(keys_ref, queries_ref, out_ref):
    out_ref[...] = SHARPNESS * contract(keys_ref[...], queries_ref[...])


def scores(keys, queries):
    return pl.pallas_call(
        scores_kernel,
        out_shape=jax.ShapeDtypeStruct((keys.shape[0], queries.shape[0]), jnp.float32),
        in_specs=[VMEM, VMEM],
        out_specs=VMEM,
        compiler_params=PARAMS,
        cost_estimate=CHEAP,
        name="scores",
    )(keys, queries)


def local_kernel(keys_ref, queries_ref, picks_ref, out_ref, chosen_ref):
    out_ref[...] = SHARPNESS * contract(keys_ref[...], queries_ref[...])
    slots, peers = picks_ref.shape
    lane = lax.broadcasted_iota(jnp.int32, (1, chosen_ref.shape[1]), 1)
    wanted = lane % TILE
    for j in range(peers * slots):
        pick = picks_ref[j % slots, member(j // slots)]
        wanted = wanted + jnp.where(lane // TILE == j, pick * TILE, 0)
    rows = lax.broadcasted_iota(jnp.int32, chosen_ref.shape, 0)
    chosen_ref[...] = (rows == wanted).astype(jnp.float32).astype(jnp.bfloat16)


def local_scores(keys, queries, picks):
    rows, hard = keys.shape[0], picks.size * TILE
    return pl.pallas_call(
        local_kernel,
        out_shape=(
            jax.ShapeDtypeStruct((rows, queries.shape[0]), jnp.float32),
            jax.ShapeDtypeStruct((rows, hard), jnp.bfloat16),
        ),
        in_specs=[VMEM, VMEM, SMEM],
        out_specs=(VMEM, VMEM),
        compiler_params=PARAMS,
        cost_estimate=CHEAP,
        name="local_scores",
    )(keys, queries, picks)


def weights_kernel(
    chunk, queries_ref, hard_ref, local_ref, near_ref, far_ref, counts_ref, positives_ref,
    grad_ref, local_out, near_out, far_out, hard_out, buffer, sems,
):
    local, near, far = local_ref[...], near_ref[...], far_ref[...]
    hard = SHARPNESS * contract(hard_ref[...], queries_ref[...])
    peers = counts_ref.shape[1]
    size = hard.shape[0] // peers
    slot = lax.broadcasted_iota(jnp.int32, (size, hard.shape[1]), 0) // TILE
    hard = jnp.concatenate(
        [
            jnp.where(slot < counts_ref[0, member(i)], hard[i * size : (i + 1) * size], -jnp.inf)
            for i in range(peers)
        ],
        axis=0,
    )
    top = lambda x: jnp.max(x, axis=0, keepdims=True)
    highest = jnp.maximum(jnp.maximum(top(local), top(near)), jnp.maximum(top(far), top(hard)))
    local, near, far = jnp.exp(local - highest), jnp.exp(near - highest), jnp.exp(far - highest)
    hard = jnp.exp(hard - highest)
    add = lambda x: jnp.sum(x, axis=0, keepdims=True)
    total = add(local) + add(near) + add(far) + add(hard)
    weight = (hard / total).astype(jnp.bfloat16)
    copies = []
    for i in range(queries_ref.shape[1] // chunk):
        columns = pl.ds(i * chunk, chunk)
        part = jnp.dot(weight, queries_ref[:, columns], preferred_element_type=jnp.float32)
        buffer[:, columns] = (SHARPNESS * part).astype(jnp.bfloat16)
        copy = pltpu.make_async_copy(buffer.at[:, columns], grad_ref.at[:, columns], sems.at[i])
        copy.start()
        copies.append(copy)
    hard_out[...] = weight
    rows = lax.broadcasted_iota(jnp.int32, local.shape, 0)
    target = (rows == positives_ref[...]).astype(jnp.float32)
    local_out[...] = (local / total - target).astype(jnp.bfloat16)
    near_out[...] = (near / total).astype(jnp.bfloat16)
    far_out[...] = (far / total).astype(jnp.bfloat16)
    for copy in copies:
        copy.wait()


def weights(queries, hard_rows, local, near, far, counts, positives, chunk=512):
    hard, width = hard_rows.shape
    like = lambda x: jax.ShapeDtypeStruct(x.shape, jnp.bfloat16)
    return pl.pallas_call(
        functools.partial(weights_kernel, chunk),
        out_shape=(
            pltpu.HBM((hard, width), jnp.bfloat16),
            like(local), like(near), like(far),
            jax.ShapeDtypeStruct((hard, queries.shape[0]), jnp.bfloat16),
        ),
        in_specs=[VMEM] * 5 + [SMEM, VMEM],
        out_specs=(HBM, VMEM, VMEM, VMEM, VMEM),
        scratch_shapes=[
            pltpu.VMEM((hard, width), jnp.bfloat16),
            pltpu.SemaphoreType.DMA((width // chunk,)),
        ],
        compiler_params=PARAMS,
        cost_estimate=CHEAP,
        name="weights",
    )(queries, hard_rows, local, near, far, counts, positives)


def pool_kernel(near_ref, far_ref, queries_ref, kept_out, sent_out):
    queries = queries_ref[...]
    far = jnp.dot(far_ref[...], queries, preferred_element_type=jnp.float32)
    sent_out[...] = (SHARPNESS * far).astype(sent_out.dtype)
    kept_out[...] = SHARPNESS * jnp.dot(near_ref[...], queries, preferred_element_type=jnp.float32)


def pool_terms(near, far, queries, link):
    shape = (near.shape[0], queries.shape[1])
    return pl.pallas_call(
        pool_kernel,
        out_shape=(jax.ShapeDtypeStruct(shape, jnp.float32), jax.ShapeDtypeStruct(shape, link)),
        in_specs=[VMEM] * 3,
        out_specs=(VMEM,) * 2,
        compiler_params=PARAMS,
        cost_estimate=CHEAP,
        name="pool_terms",
    )(near, far, queries)


def join_kernel(kept_ref, sent_ref, own_out, *piece_outs):
    size = own_out.shape[0]
    for m, out in enumerate((own_out,) + piece_outs):
        rows = pl.ds(m * size, size)
        out[...] = (kept_ref[rows] + sent_ref[rows].astype(jnp.float32)).astype(out.dtype)


def join(kept, sent, count, link):
    shape = (kept.shape[0] // count, kept.shape[1])
    return pl.pallas_call(
        join_kernel,
        out_shape=(jax.ShapeDtypeStruct(shape, jnp.float32),)
        + (jax.ShapeDtypeStruct(shape, link),) * (count - 1),
        in_specs=[VMEM] * 2,
        out_specs=(VMEM,) * count,
        compiler_params=PARAMS,
        cost_estimate=CHEAP,
        name="join",
    )(kept, sent)


def queries_kernel(
    chunk, hard_weight_ref, local_ref, near_ref, far_ref, hard_ref, passages_ref, pool_near_ref,
    pool_far_ref, out_ref, held, buffer, load_sems, store_sems,
):
    spans = [pl.ds(i * chunk, chunk) for i in range(out_ref.shape[1] // chunk)]
    loads, start = [], 0
    for k, key in enumerate((passages_ref, pool_near_ref, pool_far_ref)):
        view = held.at[pl.ds(start, key.shape[0])]
        start += key.shape[0]
        loads.append(
            [
                pltpu.make_async_copy(key.at[:, span], view.at[:, span], load_sems.at[k, i])
                for i, span in enumerate(spans)
            ]
        )
    for i in range(len(spans)):
        for load in loads:
            load[i].start()
    turned = lambda x: x.astype(jnp.float32).T.astype(jnp.bfloat16)
    hard_weight = turned(hard_weight_ref[...])
    weight = turned(jnp.concatenate([local_ref[...], near_ref[...], far_ref[...]], axis=0))
    stores = []
    for i, span in enumerate(spans):
        part = jnp.dot(hard_weight, hard_ref[:, span], preferred_element_type=jnp.float32)
        for load in loads:
            load[i].wait()
        part = part + jnp.dot(weight, held[:, span], preferred_element_type=jnp.float32)
        buffer[:, span] = (SHARPNESS * part).astype(jnp.bfloat16)
        store = pltpu.make_async_copy(buffer.at[:, span], out_ref.at[:, span], store_sems.at[i])
        store.start()
        stores.append(store)
    for store in stores:
        store.wait()


def query_gradient(hard_weight, weight, hard_rows, keys, chunk=2048):
    rows, width = hard_weight.shape[1], hard_rows.shape[1]
    return pl.pallas_call(
        functools.partial(queries_kernel, chunk),
        out_shape=pltpu.HBM((rows, width), jnp.bfloat16),
        in_specs=[VMEM] * 5 + [HBM] * 3,
        out_specs=HBM,
        scratch_shapes=[
            pltpu.VMEM((sum(key.shape[0] for key in keys), width), jnp.bfloat16),
            pltpu.VMEM((rows, width), jnp.bfloat16),
            pltpu.SemaphoreType.DMA((len(keys), width // chunk)),
            pltpu.SemaphoreType.DMA((width // chunk,)),
        ],
        compiler_params=PARAMS,
        cost_estimate=CHEAP,
        name="query_gradient",
    )(
        hard_weight, *weight, hard_rows,
        *[pltpu.with_memory_space_constraint(key, pltpu.HBM) for key in keys],
    )


def passages_kernel(
    chunk, weight_ref, queries_ref, chosen_ref, returned_ref, out_ref,
    incoming, buffer, load_sems, store_sems,
):
    spans = [pl.ds(i * chunk, chunk) for i in range(out_ref.shape[1] // chunk)]
    loads = [
        pltpu.make_async_copy(returned_ref.at[:, span], incoming.at[:, span], load_sems.at[i])
        for i, span in enumerate(spans)
    ]
    for load in loads:
        load.start()
    weight = weight_ref[...]
    chosen = chosen_ref[...]
    stores = []
    for i, span in enumerate(spans):
        part = SHARPNESS * jnp.dot(
            weight, queries_ref[:, span], preferred_element_type=jnp.float32
        )
        loads[i].wait()
        part = part + jnp.dot(chosen, incoming[:, span], preferred_element_type=jnp.float32)
        buffer[:, span] = part.astype(jnp.bfloat16)
        store = pltpu.make_async_copy(buffer.at[:, span], out_ref.at[:, span], store_sems.at[i])
        store.start()
        stores.append(store)
    for store in stores:
        store.wait()


def passage_gradient(weight, queries, chosen, returned, chunk=2048):
    rows, width = weight.shape[0], queries.shape[1]
    return pl.pallas_call(
        functools.partial(passages_kernel, chunk),
        out_shape=jax.ShapeDtypeStruct((rows, width), jnp.bfloat16),
        in_specs=[VMEM] * 3 + [HBM],
        out_specs=HBM,
        scratch_shapes=[
            pltpu.VMEM(returned.shape, jnp.bfloat16),
            pltpu.VMEM((rows, width), jnp.bfloat16),
            pltpu.SemaphoreType.DMA((width // chunk,)),
            pltpu.SemaphoreType.DMA((width // chunk,)),
        ],
        compiler_params=PARAMS,
        cost_estimate=CHEAP,
        name="passage_gradient",
    )(weight, queries, chosen, pltpu.with_memory_space_constraint(returned, pltpu.HBM))


def body(digits, queries, passages, pool_passages, positives, tile_ids, tile_count):
    rows, width = queries.shape
    picks = tile_ids[0, 0]
    peers, slots = picks.shape
    hard = peers * slots * TILE
    outgoing = gather_tiles(picks.T, passages.reshape(rows // TILE, TILE, width))
    hard_rows = trade(outgoing.reshape(peers, slots * TILE, width)).reshape(hard, width)
    pooled = pool_passages
    for step, count in digits[:-1]:
        pooled = jnp.concatenate(
            [pooled] + [shifts(pooled, ((step, count, m),), -1) for m in range(1, count)], axis=0
        )
    near = pooled
    far = shifts(near, (digits[-1] + (1,),), -1)
    local, chosen = local_scores(passages, queries, picks.T)
    grad_hard, local_weight, near_weight, far_weight, hard_weight = weights(
        queries, hard_rows, local, scores(near, queries), scores(far, queries),
        tile_count[0], positives[None, :],
    )
    returned = trade(grad_hard.reshape(peers, slots * TILE, width)).reshape(hard, width)
    *y_digits, (x_step, x_count), (core_step, core_count) = digits
    kept, sent = pool_terms(near_weight, far_weight, queries, jnp.float32)
    sent = shifts(sent, ((core_step, core_count, 1),), 1)
    term, *pieces = join(kept, sent, x_count, jnp.bfloat16)
    size = term.shape[0]
    for m, piece in enumerate(pieces, 1):
        term = term + shifts(piece, ((x_step, x_count, m),), 1).astype(jnp.float32)
    (low_step, low_count), (high_step, high_count) = y_digits
    moves = [(low, high) for high in range(high_count) for low in range(low_count)]
    size = size // len(moves)
    pieces = [term[m * size : (m + 1) * size] for m in range(len(moves))]
    term = pieces[0]
    for piece, (low, high) in zip(pieces[1:], moves[1:]):
        pair = ((low_step, low_count, low), (high_step, high_count, high))
        term = term + shifts(piece, pair, 1)
    grad_pool = term.astype(jnp.bfloat16)
    grad_queries = query_gradient(
        hard_weight, (local_weight, near_weight, far_weight), hard_rows, (passages, near, far)
    )
    grad_passages = passage_gradient(local_weight, queries, chosen, returned)
    return (grad_queries, grad_passages, grad_pool)


def solution(mesh):
    digits = ((8, 4), (32, 2), (2, 4), (1, 2))
    return jax.shard_map(
        lambda *args: body(digits, *args),
        mesh=mesh,
        in_specs=(
            P(("pb", "pool"), None),
            P(("pb", "pool"), None),
            P(("pb", "pool"), None),
            P(("pb", "pool")),
            P("pb", "pool", None, None),
            P("pb", "pool", None),
        ),
        out_specs=(P(("pb", "pool"), None), P(("pb", "pool"), None), P(("pb", "pool"), None)),
        check_vma=False,
    )
```

```python
import functools

import jax
import jax.numpy as jnp
from jax import lax
from jax.experimental import pallas as pl
from jax.experimental.pallas import tpu as pltpu
from jax.sharding import PartitionSpec as P

TILE = 8

ORDER = (0, 6, 1, 7, 2, 8, 3, 9, 4, 10, 5, 11)

SHARPNESS = 50.0

VMEM = pl.BlockSpec(memory_space=pltpu.VMEM)
SMEM = pl.BlockSpec(memory_space=pltpu.SMEM)
HBM = pl.BlockSpec(memory_space=pltpu.HBM)
PARAMS = pltpu.CompilerParams(vmem_limit_bytes=8 << 20)
CHEAP = pl.CostEstimate(flops=1 << 20, bytes_accessed=1 << 20, transcendentals=0)


def contract(left, right):
    return lax.dot_general(
        left, right, (((1,), (1,)), ((), ())), preferred_element_type=jnp.float32
    )


def transposed(left, right):
    return lax.dot_general(
        left, right, (((0,), (0,)), ((), ())), preferred_element_type=jnp.float32
    )


def trade(blocks):
    size = lax.axis_size("pool")
    groups = [[z * size + p for z in ORDER] for p in range(size)]
    return lax.all_to_all(
        blocks, ("pb", "pool"), split_axis=0, concat_axis=0, tiled=True, axis_index_groups=groups
    )


def shifts(block, moves, sign):
    def moved(j):
        for step, count, move in moves:
            digit = j // step % count
            j += ((digit + sign * move) % count - digit) * step
        return j

    return lax.ppermute(block, "pool", [(j, moved(j)) for j in range(lax.axis_size("pool"))])


def gather_kernel(
    parts, picks_ref, tiles_ref, out_ref, picks, buffer, picks_sem, load_sems, store_sems
):
    read = pltpu.make_async_copy(picks_ref, picks, picks_sem)
    read.start()
    size = tiles_ref.shape[0] // parts
    loads = []
    for i in range(parts):
        span = pl.ds(i * size, size)
        loads.append(pltpu.make_async_copy(tiles_ref.at[span], buffer.at[span], load_sems.at[i]))
        loads[-1].start()
    read.wait()
    for load in loads:
        load.wait()
    slots, peers = picks_ref.shape
    stores = []
    for j in range(peers * slots):
        tile = buffer.at[picks[j % slots, ORDER[j // slots]]]
        stores.append(pltpu.make_async_copy(tile, out_ref.at[j], store_sems.at[j]))
        stores[-1].start()
    for store in stores:
        store.wait()


def gather_tiles(picks, tiles, parts=4):
    slots, peers = picks.shape
    shape = (peers * slots,) + tiles.shape[1:]
    return pl.pallas_call(
        functools.partial(gather_kernel, parts),
        out_shape=pltpu.HBM(shape, tiles.dtype),
        in_specs=[HBM, HBM],
        out_specs=HBM,
        scratch_shapes=[
            pltpu.SMEM(picks.shape, picks.dtype),
            pltpu.VMEM(tiles.shape, tiles.dtype),
            pltpu.SemaphoreType.DMA,
            pltpu.SemaphoreType.DMA((parts,)),
            pltpu.SemaphoreType.DMA((peers * slots,)),
        ],
        compiler_params=PARAMS,
        cost_estimate=pl.CostEstimate(flops=0, bytes_accessed=3 << 20, transcendentals=0),
        name="gather_tiles",
    )(
        pltpu.with_memory_space_constraint(picks, pltpu.HBM),
        pltpu.with_memory_space_constraint(tiles, pltpu.HBM),
    )


def scores_kernel(keys_ref, queries_ref, out_ref):
    out_ref[...] = SHARPNESS * contract(keys_ref[...], queries_ref[...])


def scores(keys, queries):
    return pl.pallas_call(
        scores_kernel,
        out_shape=jax.ShapeDtypeStruct((keys.shape[0], queries.shape[0]), jnp.float32),
        in_specs=[VMEM, VMEM],
        out_specs=VMEM,
        compiler_params=PARAMS,
        cost_estimate=CHEAP,
        name="scores",
    )(keys, queries)


def local_kernel(keys_ref, queries_ref, picks_ref, out_ref, chosen_ref):
    out_ref[...] = SHARPNESS * contract(keys_ref[...], queries_ref[...])
    slots, peers = picks_ref.shape
    lane = lax.broadcasted_iota(jnp.int32, (1, chosen_ref.shape[1]), 1)
    wanted = lane % TILE
    for j in range(peers * slots):
        pick = picks_ref[j % slots, ORDER[j // slots]]
        wanted = wanted + jnp.where(lane // TILE == j, pick * TILE, 0)
    rows = lax.broadcasted_iota(jnp.int32, chosen_ref.shape, 0)
    chosen_ref[...] = (rows == wanted).astype(jnp.float32).astype(jnp.bfloat16)


def local_scores(keys, queries, picks):
    rows, hard = keys.shape[0], picks.size * TILE
    return pl.pallas_call(
        local_kernel,
        out_shape=(
            jax.ShapeDtypeStruct((rows, queries.shape[0]), jnp.float32),
            jax.ShapeDtypeStruct((rows, hard), jnp.bfloat16),
        ),
        in_specs=[VMEM, VMEM, SMEM],
        out_specs=(VMEM, VMEM),
        compiler_params=PARAMS,
        cost_estimate=CHEAP,
        name="local_scores",
    )(keys, queries, picks)


def weights_kernel(
    chunk, queries_ref, hard_ref, local_ref, near_ref, far_ref, counts_ref, positives_ref,
    grad_ref, local_out, near_out, far_out, hard_out, buffer, sems,
):
    local, near, far = local_ref[...], near_ref[...], far_ref[...]
    hard = SHARPNESS * contract(hard_ref[...], queries_ref[...])
    peers = counts_ref.shape[1]
    size = hard.shape[0] // peers
    slot = lax.broadcasted_iota(jnp.int32, (size, hard.shape[1]), 0) // TILE
    hard = jnp.concatenate(
        [
            jnp.where(slot < counts_ref[0, ORDER[i]], hard[i * size : (i + 1) * size], -jnp.inf)
            for i in range(peers)
        ],
        axis=0,
    )
    top = lambda x: jnp.max(x, axis=0, keepdims=True)
    highest = jnp.maximum(jnp.maximum(top(local), top(near)), jnp.maximum(top(far), top(hard)))
    local, near, far = jnp.exp(local - highest), jnp.exp(near - highest), jnp.exp(far - highest)
    hard = jnp.exp(hard - highest)
    add = lambda x: jnp.sum(x, axis=0, keepdims=True)
    total = add(local) + add(near) + add(far) + add(hard)
    weight = (hard / total).astype(jnp.bfloat16)
    copies = []
    for i in range(queries_ref.shape[1] // chunk):
        columns = pl.ds(i * chunk, chunk)
        part = jnp.dot(weight, queries_ref[:, columns], preferred_element_type=jnp.float32)
        buffer[:, columns] = (SHARPNESS * part).astype(jnp.bfloat16)
        copy = pltpu.make_async_copy(buffer.at[:, columns], grad_ref.at[:, columns], sems.at[i])
        copy.start()
        copies.append(copy)
    hard_out[...] = weight
    rows = lax.broadcasted_iota(jnp.int32, local.shape, 0)
    target = (rows == positives_ref[...]).astype(jnp.float32)
    local_out[...] = (local / total - target).astype(jnp.bfloat16)
    near_out[...] = (near / total).astype(jnp.bfloat16)
    far_out[...] = (far / total).astype(jnp.bfloat16)
    for copy in copies:
        copy.wait()


def weights(queries, hard_rows, local, near, far, counts, positives, chunk=512):
    hard, width = hard_rows.shape
    like = lambda x: jax.ShapeDtypeStruct(x.shape, jnp.bfloat16)
    return pl.pallas_call(
        functools.partial(weights_kernel, chunk),
        out_shape=(
            pltpu.HBM((hard, width), jnp.bfloat16),
            like(local), like(near), like(far),
            jax.ShapeDtypeStruct((hard, queries.shape[0]), jnp.bfloat16),
        ),
        in_specs=[VMEM] * 5 + [SMEM, VMEM],
        out_specs=(HBM, VMEM, VMEM, VMEM, VMEM),
        scratch_shapes=[
            pltpu.VMEM((hard, width), jnp.bfloat16),
            pltpu.SemaphoreType.DMA((width // chunk,)),
        ],
        compiler_params=PARAMS,
        cost_estimate=CHEAP,
        name="weights",
    )(queries, hard_rows, local, near, far, counts, positives)


def pool_kernel(near_ref, far_ref, queries_ref, kept_out, sent_out):
    queries = queries_ref[...]
    far = jnp.dot(far_ref[...], queries, preferred_element_type=jnp.float32)
    sent_out[...] = (SHARPNESS * far).astype(sent_out.dtype)
    kept_out[...] = SHARPNESS * jnp.dot(near_ref[...], queries, preferred_element_type=jnp.float32)


def pool_terms(near, far, queries, link):
    shape = (near.shape[0], queries.shape[1])
    return pl.pallas_call(
        pool_kernel,
        out_shape=(jax.ShapeDtypeStruct(shape, jnp.float32), jax.ShapeDtypeStruct(shape, link)),
        in_specs=[VMEM] * 3,
        out_specs=(VMEM,) * 2,
        compiler_params=PARAMS,
        cost_estimate=CHEAP,
        name="pool_terms",
    )(near, far, queries)


def join_kernel(kept_ref, sent_ref, own_out, *piece_outs):
    size = own_out.shape[0]
    for m, out in enumerate((own_out,) + piece_outs):
        rows = pl.ds(m * size, size)
        out[...] = (kept_ref[rows] + sent_ref[rows].astype(jnp.float32)).astype(out.dtype)


def join(kept, sent, count, link):
    shape = (kept.shape[0] // count, kept.shape[1])
    return pl.pallas_call(
        join_kernel,
        out_shape=(jax.ShapeDtypeStruct(shape, jnp.float32),)
        + (jax.ShapeDtypeStruct(shape, link),) * (count - 1),
        in_specs=[VMEM] * 2,
        out_specs=(VMEM,) * count,
        compiler_params=PARAMS,
        cost_estimate=CHEAP,
        name="join",
    )(kept, sent)


def queries_kernel(
    chunk, hard_weight_ref, local_ref, near_ref, far_ref, hard_ref, passages_ref, pool_near_ref,
    pool_far_ref, out_ref, held, buffer, load_sems, store_sems,
):
    spans = [pl.ds(i * chunk, chunk) for i in range(out_ref.shape[1] // chunk)]
    loads, start = [], 0
    for k, key in enumerate((passages_ref, pool_near_ref, pool_far_ref)):
        view = held.at[pl.ds(start, key.shape[0])]
        start += key.shape[0]
        loads.append(
            [
                pltpu.make_async_copy(key.at[:, span], view.at[:, span], load_sems.at[k, i])
                for i, span in enumerate(spans)
            ]
        )
    for i in range(len(spans)):
        for load in loads:
            load[i].start()
    turned = lambda x: x.astype(jnp.float32).T.astype(jnp.bfloat16)
    hard_weight = turned(hard_weight_ref[...])
    weight = turned(jnp.concatenate([local_ref[...], near_ref[...], far_ref[...]], axis=0))
    stores = []
    for i, span in enumerate(spans):
        part = jnp.dot(hard_weight, hard_ref[:, span], preferred_element_type=jnp.float32)
        for load in loads:
            load[i].wait()
        part = part + jnp.dot(weight, held[:, span], preferred_element_type=jnp.float32)
        buffer[:, span] = (SHARPNESS * part).astype(jnp.bfloat16)
        store = pltpu.make_async_copy(buffer.at[:, span], out_ref.at[:, span], store_sems.at[i])
        store.start()
        stores.append(store)
    for store in stores:
        store.wait()


def query_gradient(hard_weight, weight, hard_rows, keys, chunk=2048):
    rows, width = hard_weight.shape[1], hard_rows.shape[1]
    return pl.pallas_call(
        functools.partial(queries_kernel, chunk),
        out_shape=pltpu.HBM((rows, width), jnp.bfloat16),
        in_specs=[VMEM] * 5 + [HBM] * 3,
        out_specs=HBM,
        scratch_shapes=[
            pltpu.VMEM((sum(key.shape[0] for key in keys), width), jnp.bfloat16),
            pltpu.VMEM((rows, width), jnp.bfloat16),
            pltpu.SemaphoreType.DMA((len(keys), width // chunk)),
            pltpu.SemaphoreType.DMA((width // chunk,)),
        ],
        compiler_params=PARAMS,
        cost_estimate=CHEAP,
        name="query_gradient",
    )(
        hard_weight, *weight, hard_rows,
        *[pltpu.with_memory_space_constraint(key, pltpu.HBM) for key in keys],
    )


def passages_kernel(
    chunk, weight_ref, queries_ref, chosen_ref, returned_ref, out_ref,
    incoming, buffer, load_sems, store_sems,
):
    spans = [pl.ds(i * chunk, chunk) for i in range(out_ref.shape[1] // chunk)]
    loads = [
        pltpu.make_async_copy(returned_ref.at[:, span], incoming.at[:, span], load_sems.at[i])
        for i, span in enumerate(spans)
    ]
    for load in loads:
        load.start()
    weight = weight_ref[...]
    chosen = chosen_ref[...]
    stores = []
    for i, span in enumerate(spans):
        part = SHARPNESS * jnp.dot(
            weight, queries_ref[:, span], preferred_element_type=jnp.float32
        )
        loads[i].wait()
        part = part + jnp.dot(chosen, incoming[:, span], preferred_element_type=jnp.float32)
        buffer[:, span] = part.astype(jnp.bfloat16)
        store = pltpu.make_async_copy(buffer.at[:, span], out_ref.at[:, span], store_sems.at[i])
        store.start()
        stores.append(store)
    for store in stores:
        store.wait()


def passage_gradient(weight, queries, chosen, returned, chunk=2048):
    rows, width = weight.shape[0], queries.shape[1]
    return pl.pallas_call(
        functools.partial(passages_kernel, chunk),
        out_shape=jax.ShapeDtypeStruct((rows, width), jnp.bfloat16),
        in_specs=[VMEM] * 3 + [HBM],
        out_specs=HBM,
        scratch_shapes=[
            pltpu.VMEM(returned.shape, jnp.bfloat16),
            pltpu.VMEM((rows, width), jnp.bfloat16),
            pltpu.SemaphoreType.DMA((width // chunk,)),
            pltpu.SemaphoreType.DMA((width // chunk,)),
        ],
        compiler_params=PARAMS,
        cost_estimate=CHEAP,
        name="passage_gradient",
    )(weight, queries, chosen, pltpu.with_memory_space_constraint(returned, pltpu.HBM))


def body(digits, queries, passages, pool_passages, positives, tile_ids, tile_count):
    rows, width = queries.shape
    picks = tile_ids[0, 0]
    peers, slots = picks.shape
    hard = peers * slots * TILE
    outgoing = gather_tiles(picks.T, passages.reshape(rows // TILE, TILE, width))
    hard_rows = trade(outgoing.reshape(peers, slots * TILE, width)).reshape(hard, width)
    pooled = pool_passages
    for step, count in digits[:-1]:
        pooled = jnp.concatenate(
            [pooled] + [shifts(pooled, ((step, count, m),), -1) for m in range(1, count)], axis=0
        )
    near = pooled
    far = shifts(near, (digits[-1] + (1,),), -1)
    local, chosen = local_scores(passages, queries, picks.T)
    grad_hard, local_weight, near_weight, far_weight, hard_weight = weights(
        queries, hard_rows, local, scores(near, queries), scores(far, queries),
        tile_count[0], positives[None, :],
    )
    returned = trade(grad_hard.reshape(peers, slots * TILE, width)).reshape(hard, width)
    *y_digits, (x_step, x_count), (core_step, core_count) = digits
    kept, sent = pool_terms(near_weight, far_weight, queries, jnp.float32)
    sent = shifts(sent, ((core_step, core_count, 1),), 1)
    term, *pieces = join(kept, sent, x_count, jnp.bfloat16)
    size = term.shape[0]
    for m, piece in enumerate(pieces, 1):
        term = term + shifts(piece, ((x_step, x_count, m),), 1).astype(jnp.float32)
    (low_step, low_count), (high_step, high_count) = y_digits
    moves = [(low, high) for high in range(high_count) for low in range(low_count)]
    size = size // len(moves)
    pieces = [term[m * size : (m + 1) * size] for m in range(len(moves))]
    term = pieces[0]
    for piece, (low, high) in zip(pieces[1:], moves[1:]):
        pair = ((low_step, low_count, low), (high_step, high_count, high))
        term = term + shifts(piece, pair, 1)
    grad_pool = term.astype(jnp.bfloat16)
    grad_queries = query_gradient(
        hard_weight, (local_weight, near_weight, far_weight), hard_rows, (passages, near, far)
    )
    grad_passages = passage_gradient(local_weight, queries, chosen, returned)
    return (grad_queries, grad_passages, grad_pool)


def solution(mesh):
    digits = ((8, 4), (32, 2), (2, 4), (1, 2))
    return jax.shard_map(
        lambda *args: body(digits, *args),
        mesh=mesh,
        in_specs=(
            P(("pb", "pool"), None),
            P(("pb", "pool"), None),
            P(("pb", "pool"), None),
            P(("pb", "pool")),
            P("pb", "pool", None, None),
            P("pb", "pool", None),
        ),
        out_specs=(P(("pb", "pool"), None), P(("pb", "pool"), None), P(("pb", "pool"), None)),
        check_vma=False,
    )
```

```python
import functools

import jax
import jax.numpy as jnp
from jax import lax
from jax.experimental import pallas as pl
from jax.experimental.pallas import tpu as pltpu
from jax.sharding import PartitionSpec as P

TILE = 8

ORDERS = ((0, 6, 1, 7, 2, 8, 3, 9, 4, 10, 5, 11), (0, 6, 3, 9, 1, 7, 4, 10, 2, 8, 5, 11))

SHARPNESS = 50.0

VMEM = pl.BlockSpec(memory_space=pltpu.VMEM)
SMEM = pl.BlockSpec(memory_space=pltpu.SMEM)
HBM = pl.BlockSpec(memory_space=pltpu.HBM)
PARAMS = pltpu.CompilerParams(vmem_limit_bytes=8 << 20)
CHEAP = pl.CostEstimate(flops=1 << 20, bytes_accessed=1 << 20, transcendentals=0)


def contract(left, right):
    return lax.dot_general(
        left, right, (((1,), (1,)), ((), ())), preferred_element_type=jnp.float32
    )


def transposed(left, right):
    return lax.dot_general(
        left, right, (((0,), (0,)), ((), ())), preferred_element_type=jnp.float32
    )


def member(k):
    first, second = ORDERS[0][k], ORDERS[1][k]
    return first + lax.axis_index("pool") % 2 * (second - first)


def trade(blocks):
    size = lax.axis_size("pool")
    groups = [[z * size + p for z in ORDERS[p % 2]] for p in range(size)]
    return lax.all_to_all(
        blocks, ("pb", "pool"), split_axis=0, concat_axis=0, tiled=True, axis_index_groups=groups
    )


def shifts(block, moves, sign):
    def moved(j):
        for step, count, move in moves:
            digit = j // step % count
            j += ((digit + sign * move) % count - digit) * step
        return j

    return lax.ppermute(block, "pool", [(j, moved(j)) for j in range(lax.axis_size("pool"))])


def gather_kernel(
    parts, picks_ref, tiles_ref, out_ref, picks, buffer, picks_sem, load_sems, store_sems
):
    read = pltpu.make_async_copy(picks_ref, picks, picks_sem)
    read.start()
    size = tiles_ref.shape[0] // parts
    loads = []
    for i in range(parts):
        span = pl.ds(i * size, size)
        loads.append(pltpu.make_async_copy(tiles_ref.at[span], buffer.at[span], load_sems.at[i]))
        loads[-1].start()
    read.wait()
    for load in loads:
        load.wait()
    slots, peers = picks_ref.shape
    stores = []
    for j in range(peers * slots):
        tile = buffer.at[picks[j % slots, member(j // slots)]]
        stores.append(pltpu.make_async_copy(tile, out_ref.at[j], store_sems.at[j]))
        stores[-1].start()
    for store in stores:
        store.wait()


def gather_tiles(picks, tiles, parts=4):
    slots, peers = picks.shape
    shape = (peers * slots,) + tiles.shape[1:]
    return pl.pallas_call(
        functools.partial(gather_kernel, parts),
        out_shape=pltpu.HBM(shape, tiles.dtype),
        in_specs=[HBM, HBM],
        out_specs=HBM,
        scratch_shapes=[
            pltpu.SMEM(picks.shape, picks.dtype),
            pltpu.VMEM(tiles.shape, tiles.dtype),
            pltpu.SemaphoreType.DMA,
            pltpu.SemaphoreType.DMA((parts,)),
            pltpu.SemaphoreType.DMA((peers * slots,)),
        ],
        compiler_params=PARAMS,
        cost_estimate=pl.CostEstimate(flops=0, bytes_accessed=3 << 20, transcendentals=0),
        name="gather_tiles",
    )(
        pltpu.with_memory_space_constraint(picks, pltpu.HBM),
        pltpu.with_memory_space_constraint(tiles, pltpu.HBM),
    )


def scores_kernel(keys_ref, queries_ref, out_ref):
    out_ref[...] = SHARPNESS * contract(keys_ref[...], queries_ref[...])


def scores(keys, queries):
    return pl.pallas_call(
        scores_kernel,
        out_shape=jax.ShapeDtypeStruct((keys.shape[0], queries.shape[0]), jnp.float32),
        in_specs=[VMEM, VMEM],
        out_specs=VMEM,
        compiler_params=PARAMS,
        cost_estimate=CHEAP,
        name="scores",
    )(keys, queries)


def local_kernel(keys_ref, queries_ref, picks_ref, out_ref, chosen_ref):
    out_ref[...] = SHARPNESS * contract(keys_ref[...], queries_ref[...])
    slots, peers = picks_ref.shape
    lane = lax.broadcasted_iota(jnp.int32, (1, chosen_ref.shape[1]), 1)
    wanted = lane % TILE
    for j in range(peers * slots):
        pick = picks_ref[j % slots, member(j // slots)]
        wanted = wanted + jnp.where(lane // TILE == j, pick * TILE, 0)
    rows = lax.broadcasted_iota(jnp.int32, chosen_ref.shape, 0)
    chosen_ref[...] = (rows == wanted).astype(jnp.float32).astype(jnp.bfloat16)


def local_scores(keys, queries, picks):
    rows, hard = keys.shape[0], picks.size * TILE
    return pl.pallas_call(
        local_kernel,
        out_shape=(
            jax.ShapeDtypeStruct((rows, queries.shape[0]), jnp.float32),
            jax.ShapeDtypeStruct((rows, hard), jnp.bfloat16),
        ),
        in_specs=[VMEM, VMEM, SMEM],
        out_specs=(VMEM, VMEM),
        compiler_params=PARAMS,
        cost_estimate=CHEAP,
        name="local_scores",
    )(keys, queries, picks)


def weights_kernel(
    chunk, queries_ref, hard_ref, local_ref, near_ref, far_ref, counts_ref, positives_ref,
    grad_ref, local_out, near_out, far_out, hard_out, buffer, sems,
):
    local, near, far = local_ref[...], near_ref[...], far_ref[...]
    hard = SHARPNESS * contract(hard_ref[...], queries_ref[...])
    peers = counts_ref.shape[1]
    size = hard.shape[0] // peers
    slot = lax.broadcasted_iota(jnp.int32, (size, hard.shape[1]), 0) // TILE
    hard = jnp.concatenate(
        [
            jnp.where(slot < counts_ref[0, member(i)], hard[i * size : (i + 1) * size], -jnp.inf)
            for i in range(peers)
        ],
        axis=0,
    )
    top = lambda x: jnp.max(x, axis=0, keepdims=True)
    highest = jnp.maximum(jnp.maximum(top(local), top(near)), jnp.maximum(top(far), top(hard)))
    local, near, far = jnp.exp(local - highest), jnp.exp(near - highest), jnp.exp(far - highest)
    hard = jnp.exp(hard - highest)
    add = lambda x: jnp.sum(x, axis=0, keepdims=True)
    total = add(local) + add(near) + add(far) + add(hard)
    weight = (hard / total).astype(jnp.bfloat16)
    copies = []
    for i in range(queries_ref.shape[1] // chunk):
        columns = pl.ds(i * chunk, chunk)
        part = jnp.dot(weight, queries_ref[:, columns], preferred_element_type=jnp.float32)
        buffer[:, columns] = (SHARPNESS * part).astype(jnp.bfloat16)
        copy = pltpu.make_async_copy(buffer.at[:, columns], grad_ref.at[:, columns], sems.at[i])
        copy.start()
        copies.append(copy)
    hard_out[...] = weight
    rows = lax.broadcasted_iota(jnp.int32, local.shape, 0)
    target = (rows == positives_ref[...]).astype(jnp.float32)
    local_out[...] = (local / total - target).astype(jnp.bfloat16)
    near_out[...] = (near / total).astype(jnp.bfloat16)
    far_out[...] = (far / total).astype(jnp.bfloat16)
    for copy in copies:
        copy.wait()


def weights(queries, hard_rows, local, near, far, counts, positives, chunk=512):
    hard, width = hard_rows.shape
    like = lambda x: jax.ShapeDtypeStruct(x.shape, jnp.bfloat16)
    return pl.pallas_call(
        functools.partial(weights_kernel, chunk),
        out_shape=(
            pltpu.HBM((hard, width), jnp.bfloat16),
            like(local), like(near), like(far),
            jax.ShapeDtypeStruct((hard, queries.shape[0]), jnp.bfloat16),
        ),
        in_specs=[VMEM] * 5 + [SMEM, VMEM],
        out_specs=(HBM, VMEM, VMEM, VMEM, VMEM),
        scratch_shapes=[
            pltpu.VMEM((hard, width), jnp.bfloat16),
            pltpu.SemaphoreType.DMA((width // chunk,)),
        ],
        compiler_params=PARAMS,
        cost_estimate=CHEAP,
        name="weights",
    )(queries, hard_rows, local, near, far, counts, positives)


def pool_kernel(near_ref, far_ref, queries_ref, kept_out, sent_out):
    queries = queries_ref[...]
    far = jnp.dot(far_ref[...], queries, preferred_element_type=jnp.float32)
    sent_out[...] = (SHARPNESS * far).astype(sent_out.dtype)
    kept_out[...] = SHARPNESS * jnp.dot(near_ref[...], queries, preferred_element_type=jnp.float32)


def pool_terms(near, far, queries, link):
    shape = (near.shape[0], queries.shape[1])
    return pl.pallas_call(
        pool_kernel,
        out_shape=(jax.ShapeDtypeStruct(shape, jnp.float32), jax.ShapeDtypeStruct(shape, link)),
        in_specs=[VMEM] * 3,
        out_specs=(VMEM,) * 2,
        compiler_params=PARAMS,
        cost_estimate=CHEAP,
        name="pool_terms",
    )(near, far, queries)


def join_kernel(kept_ref, sent_ref, own_out, *piece_outs):
    size = own_out.shape[0]
    for m, out in enumerate((own_out,) + piece_outs):
        rows = pl.ds(m * size, size)
        out[...] = (kept_ref[rows] + sent_ref[rows].astype(jnp.float32)).astype(out.dtype)


def join(kept, sent, count, link):
    shape = (kept.shape[0] // count, kept.shape[1])
    return pl.pallas_call(
        join_kernel,
        out_shape=(jax.ShapeDtypeStruct(shape, jnp.float32),)
        + (jax.ShapeDtypeStruct(shape, link),) * (count - 1),
        in_specs=[VMEM] * 2,
        out_specs=(VMEM,) * count,
        compiler_params=PARAMS,
        cost_estimate=CHEAP,
        name="join",
    )(kept, sent)


def queries_kernel(
    chunk, hard_weight_ref, local_ref, near_ref, far_ref, hard_ref, passages_ref, pool_near_ref,
    pool_far_ref, out_ref, held, buffer, load_sems, store_sems,
):
    spans = [pl.ds(i * chunk, chunk) for i in range(out_ref.shape[1] // chunk)]
    loads, start = [], 0
    for k, key in enumerate((passages_ref, pool_near_ref, pool_far_ref)):
        view = held.at[pl.ds(start, key.shape[0])]
        start += key.shape[0]
        loads.append(
            [
                pltpu.make_async_copy(key.at[:, span], view.at[:, span], load_sems.at[k, i])
                for i, span in enumerate(spans)
            ]
        )
    for i in range(len(spans)):
        for load in loads:
            load[i].start()
    turned = lambda x: x.astype(jnp.float32).T.astype(jnp.bfloat16)
    hard_weight = turned(hard_weight_ref[...])
    weight = turned(jnp.concatenate([local_ref[...], near_ref[...], far_ref[...]], axis=0))
    stores = []
    for i, span in enumerate(spans):
        part = jnp.dot(hard_weight, hard_ref[:, span], preferred_element_type=jnp.float32)
        for load in loads:
            load[i].wait()
        part = part + jnp.dot(weight, held[:, span], preferred_element_type=jnp.float32)
        buffer[:, span] = (SHARPNESS * part).astype(jnp.bfloat16)
        store = pltpu.make_async_copy(buffer.at[:, span], out_ref.at[:, span], store_sems.at[i])
        store.start()
        stores.append(store)
    for store in stores:
        store.wait()


def query_gradient(hard_weight, weight, hard_rows, keys, chunk=2048):
    rows, width = hard_weight.shape[1], hard_rows.shape[1]
    return pl.pallas_call(
        functools.partial(queries_kernel, chunk),
        out_shape=pltpu.HBM((rows, width), jnp.bfloat16),
        in_specs=[VMEM] * 5 + [HBM] * 3,
        out_specs=HBM,
        scratch_shapes=[
            pltpu.VMEM((sum(key.shape[0] for key in keys), width), jnp.bfloat16),
            pltpu.VMEM((rows, width), jnp.bfloat16),
            pltpu.SemaphoreType.DMA((len(keys), width // chunk)),
            pltpu.SemaphoreType.DMA((width // chunk,)),
        ],
        compiler_params=PARAMS,
        cost_estimate=CHEAP,
        name="query_gradient",
    )(
        hard_weight, *weight, hard_rows,
        *[pltpu.with_memory_space_constraint(key, pltpu.HBM) for key in keys],
    )


def passages_kernel(
    chunk, weight_ref, queries_ref, chosen_ref, returned_ref, out_ref,
    incoming, buffer, load_sems, store_sems,
):
    spans = [pl.ds(i * chunk, chunk) for i in range(out_ref.shape[1] // chunk)]
    loads = [
        pltpu.make_async_copy(returned_ref.at[:, span], incoming.at[:, span], load_sems.at[i])
        for i, span in enumerate(spans)
    ]
    for load in loads:
        load.start()
    weight = weight_ref[...]
    chosen = chosen_ref[...]
    stores = []
    for i, span in enumerate(spans):
        part = SHARPNESS * jnp.dot(
            weight, queries_ref[:, span], preferred_element_type=jnp.float32
        )
        loads[i].wait()
        part = part + jnp.dot(chosen, incoming[:, span], preferred_element_type=jnp.float32)
        buffer[:, span] = part.astype(jnp.bfloat16)
        store = pltpu.make_async_copy(buffer.at[:, span], out_ref.at[:, span], store_sems.at[i])
        store.start()
        stores.append(store)
    for store in stores:
        store.wait()


def passage_gradient(weight, queries, chosen, returned, chunk=2048):
    rows, width = weight.shape[0], queries.shape[1]
    return pl.pallas_call(
        functools.partial(passages_kernel, chunk),
        out_shape=jax.ShapeDtypeStruct((rows, width), jnp.bfloat16),
        in_specs=[VMEM] * 3 + [HBM],
        out_specs=HBM,
        scratch_shapes=[
            pltpu.VMEM(returned.shape, jnp.bfloat16),
            pltpu.VMEM((rows, width), jnp.bfloat16),
            pltpu.SemaphoreType.DMA((width // chunk,)),
            pltpu.SemaphoreType.DMA((width // chunk,)),
        ],
        compiler_params=PARAMS,
        cost_estimate=CHEAP,
        name="passage_gradient",
    )(weight, queries, chosen, pltpu.with_memory_space_constraint(returned, pltpu.HBM))


def body(digits, queries, passages, pool_passages, positives, tile_ids, tile_count):
    rows, width = queries.shape
    picks = tile_ids[0, 0]
    peers, slots = picks.shape
    hard = peers * slots * TILE
    outgoing = gather_tiles(picks.T, passages.reshape(rows // TILE, TILE, width))
    hard_rows = trade(outgoing.reshape(peers, slots * TILE, width)).reshape(hard, width)
    pooled = pool_passages
    for step, count in digits[:-1]:
        pooled = jnp.concatenate(
            [pooled] + [shifts(pooled, ((step, count, m),), -1) for m in range(1, count)], axis=0
        )
    near = pooled
    far = shifts(near, (digits[-1] + (1,),), -1)
    local, chosen = local_scores(passages, queries, picks.T)
    grad_hard, local_weight, near_weight, far_weight, hard_weight = weights(
        queries, hard_rows, local, scores(near, queries), scores(far, queries),
        tile_count[0], positives[None, :],
    )
    returned = trade(grad_hard.reshape(peers, slots * TILE, width)).reshape(hard, width)
    *y_digits, (x_step, x_count), (core_step, core_count) = digits
    kept, sent = pool_terms(near_weight, far_weight, queries, jnp.float32)
    sent = shifts(sent, ((core_step, core_count, 1),), 1)
    term, *pieces = join(kept, sent, x_count, jnp.bfloat16)
    size = term.shape[0]
    for m, piece in enumerate(pieces, 1):
        term = term + shifts(piece, ((x_step, x_count, m),), 1).astype(jnp.float32)
    (low_step, low_count), (high_step, high_count) = y_digits
    moves = [(low, high) for high in range(high_count) for low in range(low_count)]
    size = size // len(moves)
    pieces = [term[m * size : (m + 1) * size] for m in range(len(moves))]
    term = pieces[0]
    for piece, (low, high) in zip(pieces[1:], moves[1:]):
        pair = ((low_step, low_count, low), (high_step, high_count, high))
        term = term + shifts(piece, pair, 1)
    grad_pool = term.astype(jnp.bfloat16)
    grad_queries = query_gradient(
        hard_weight, (local_weight, near_weight, far_weight), hard_rows, (passages, near, far)
    )
    grad_passages = passage_gradient(local_weight, queries, chosen, returned)
    return (grad_queries, grad_passages, grad_pool)


def solution(mesh):
    digits = ((8, 4), (32, 2), (2, 4), (1, 2))
    return jax.shard_map(
        lambda *args: body(digits, *args),
        mesh=mesh,
        in_specs=(
            P(("pb", "pool"), None),
            P(("pb", "pool"), None),
            P(("pb", "pool"), None),
            P(("pb", "pool")),
            P("pb", "pool", None, None),
            P("pb", "pool", None),
        ),
        out_specs=(P(("pb", "pool"), None), P(("pb", "pool"), None), P(("pb", "pool"), None)),
        check_vma=False,
    )
```
